128 devices in a mesh: tile: 128 (over y, x, z, core).
Axes of the slice: x: 4, y: 4, z: 4, core: 2. Of those that a mesh axis runs over, the one named last changes fastest.
Arguments:
- features: bfloat16 [128, 16, 16, 128], P('tile'), may hold values from -6 to 6
- cotangent: bfloat16 [128, 16, 16, 128], P('tile'), may hold values from -6 to 6
- kernel_first_layer: bfloat16 [3, 3, 128, 128], replicated, may hold values from -0.1875 to 0.1875
- kernel_second_layer: bfloat16 [3, 3, 128, 128], replicated, may hold values from -0.1875 to 0.1875
- neighbors: int32 [128, 8], replicated, may hold values from -1 to 127, as said below
- turns: int32 [128, 8], replicated, may hold values from 0 to 3, as said below
Outputs:
- output: bfloat16 [128, 16, 16, 128], P('tile')
- features_gradient: bfloat16 [128, 16, 16, 128], P('tile')
- first_kernel_gradient: float32 [3, 3, 128, 128], replicated
- second_kernel_gradient: float32 [3, 3, 128, 128], replicated
The draws below stay inside these ranges and needn't reach their ends.
Inputs may be any that keep to these rules, and one draw needn't show every extreme that they name: `neighbors`: entry (t, d) is the tile beside tile t in direction d (0 to 7: north, north-east, east, south-east, south, south-west, west, north-west), or -1 where there is none; -1 occurs only in the four diagonal directions; the entries of one row other than -1 are distinct and differ from t. Entry (t, d) is the number of counter-clockwise quarter turns that bring the tile neighbors[t, d] into tile t's orientation; it is 0 where neighbors[t, d] is -1.
All inputs are finite; a program needn't handle non-finite values.
Results may differ from the reference program's by a relative error of at most 0.0059.
Values may be sent and summed in bfloat16 or wider, within the bound.
A program may use at most 64 MiB of HBM per device.

```python
import math
import jax
import jax.numpy as jnp
from jax import lax

CH = 128
SIDE = 16
FIRST_SPACING = 1
SECOND_SPACING = 2
TILES = 128


def tile_graph(key):
    face_rows = TILES // 16
    face_cols = 8
    face_size = face_rows * face_cols
    geometry = jnp.arange(TILES, dtype=jnp.int32)
    face_of = geometry // face_size
    row_of = geometry // face_cols % face_rows
    col_of = geometry % face_cols
    row_step = jnp.array([-1, -1, 0, 1, 1, 1, 0, -1], dtype=jnp.int32)
    col_step = jnp.array([0, 1, 1, 1, 0, -1, -1, -1], dtype=jnp.int32)
    new_row = row_of[:, None] + row_step[None, :]
    new_col = col_of[:, None] + col_step[None, :]
    row_inside = (new_row >= 0) & (new_row < face_rows)
    col_inside = (new_col >= 0) & (new_col < face_cols)
    same_face = face_of[:, None] * face_size + jnp.clip(new_row, 0, face_rows - 1) * face_cols + new_col % face_cols
    pole_row = jnp.where(new_row < 0, 0, face_rows - 1)
    other_face = (1 - face_of[:, None]) * face_size + pole_row * face_cols + (face_cols - 1 - jnp.clip(new_col, 0, face_cols - 1))
    geo_partner = jnp.where(row_inside, same_face, jnp.where(col_inside, other_face, -1))
    crossing_turns = jax.random.permutation(jax.random.fold_in(key, 11), 4).astype(jnp.int32)
    crossing_code = 2 * face_of[:, None] + (new_row >= face_rows).astype(jnp.int32)
    geo_turn = jnp.where(row_inside, 0, jnp.where(col_inside, crossing_turns[crossing_code], 0))
    placement = jax.random.permutation(jax.random.fold_in(key, 12), TILES).astype(jnp.int32)
    partner_device = jnp.where(geo_partner >= 0, placement[jnp.maximum(geo_partner, 0)], -1)
    neighbor_table = jnp.zeros((TILES, 8), jnp.int32).at[placement].set(partner_device.astype(jnp.int32))
    turn_table = jnp.zeros((TILES, 8), jnp.int32).at[placement].set(geo_turn.astype(jnp.int32))
    return (neighbor_table, turn_table)


def draw_neighbors(key, part):
    return tile_graph(key)[0]


def draw_turns(key, part):
    return tile_graph(key)[1]


def block_scale(key, shape, pieces, low, top_value):
    loudness, own = 1.0, jax.random.fold_in(key, 6)
    for axis_at, parts in pieces:
        heights = jnp.exp(jax.random.uniform(jax.random.fold_in(own, axis_at), (parts,), jnp.float32, low / len(pieces), top_value / len(pieces)))
        loudness = loudness * jnp.repeat(heights, shape[axis_at] // parts).reshape([-1 if axis == axis_at else 1 for axis in range(len(shape))])
    return loudness


def normal_values(rng, dims, scale, most, split=(), kind=jnp.bfloat16):
    values = scale * jax.random.normal(rng, dims, jnp.float32)
    if split:
        values = values * block_scale(rng, dims, split, -0.22, 0.18)
    return jnp.clip(values, -most, most).astype(kind)


def setup_inputs(seed: int = 0) -> dict:
    key_of = jax.random.split(jax.random.key(seed), 7)
    features = normal_values(key_of[0], (TILES, SIDE, SIDE, CH), 1.0, 6.0, ((0, 128),))
    cotangent = normal_values(key_of[1], (TILES, SIDE, SIDE, CH), 1.0, 6.0, ((0, 128),))
    kernel_first_layer = normal_values(key_of[2], (3, 3, CH, CH), (9 * CH) ** -0.5, 0.1875)
    kernel_second_layer = normal_values(key_of[3], (3, 3, CH, CH), (9 * CH) ** -0.5, 0.1875)
    neighbors = draw_neighbors(jax.random.fold_in(key_of[6], 71), 0)
    turns = draw_turns(jax.random.fold_in(key_of[6], 71), 0)
    return {"features": features, "cotangent": cotangent, "kernel_first_layer": kernel_first_layer, "kernel_second_layer": kernel_second_layer, "neighbors": neighbors, "turns": turns}


gelu_scale = 0.7978845608028654
gelu_cubic = 0.044715

def strip_slices(tile_side, compass, rim_width):
    head_part = slice(0, rim_width)
    tail_part = slice(tile_side - rim_width, tile_side)
    whole_span = slice(0, tile_side)
    row_pick = (head_part, head_part, whole_span, tail_part, tail_part, tail_part, whole_span, head_part)[compass]
    col_pick = (whole_span, tail_part, tail_part, tail_part, whole_span, head_part, head_part, head_part)[compass]
    return (row_pick, col_pick)

def strip_of(strip_block, compass, rim_width):
    row_pick, col_pick = strip_slices(strip_block.shape[-2], compass, rim_width)
    return strip_block[..., row_pick, col_pick, :]

def turned(strip_block, quarter):
    return jnp.rot90(strip_block, quarter, axes=(strip_block.ndim - 3, strip_block.ndim - 2))

def select_quarter(variants, quarter_code):
    result = variants[0]
    for quarter in range(1, 4):
        result = jnp.where(quarter_code == quarter, variants[quarter], result)
    return result

def assemble(center, regions):
    top_band = jnp.concatenate([regions[7], regions[0], regions[1]], axis=-2)
    middle = jnp.concatenate([regions[6], center, regions[2]], axis=-2)
    bottom = jnp.concatenate([regions[5], regions[4], regions[3]], axis=-2)
    return jnp.concatenate([top_band, middle, bottom], axis=-3)

def margin_everywhere(tiles, neighbors, turns, rim_width):
    regions = []
    for direction in range(8):
        source = neighbors[:, direction]
        safe_source = jnp.maximum(source, 0).astype(jnp.int32)
        variants = []
        for quarter in range(4):
            strips = strip_of(tiles, (direction + 4 + 2 * quarter) % 8, rim_width)
            variants.append(turned(jnp.take(strips, safe_source, axis=0), quarter))
        region = select_quarter(variants, turns[:, direction][:, None, None, None])
        present = (source >= 0)[:, None, None, None]
        regions.append(jnp.where(present, region, jnp.zeros_like(region)))
    return assemble(tiles, regions)

def margin_transpose(grad_padded, neighbors, turns, rim_width):
    tile_side = grad_padded.shape[1] - 2 * rim_width
    zero_tiles = jnp.zeros((grad_padded.shape[0], tile_side, tile_side, grad_padded.shape[3]), grad_padded.dtype)

    def linear_map(tiles):
        return margin_everywhere(tiles, neighbors, turns, rim_width)
    primal_out, pullback = jax.vjp(linear_map, zero_tiles)
    return pullback(grad_padded)[0]

def gelu_pair(preactivation):
    tanh_arg = gelu_scale * (preactivation + gelu_cubic * preactivation * preactivation * preactivation)
    tangent = jnp.tanh(tanh_arg)
    activated = 0.5 * preactivation * (1.0 + tangent)
    derivative = 0.5 * (1.0 + tangent) + 0.5 * preactivation * (1.0 - tangent * tangent) * gelu_scale * (1.0 + 3.0 * gelu_cubic * preactivation * preactivation)
    return (activated, derivative)

def apply_convolution(padded, kernel, dilation):
    return lax.conv_general_dilated(padded, kernel, (1, 1), 'VALID', rhs_dilation=(dilation, dilation), dimension_numbers=('NHWC', 'HWIO', 'NHWC'), precision=lax.Precision.HIGHEST, preferred_element_type=jnp.float32)

def convolution_backward(cotangent, kernel, dilation):
    margin = 2 * dilation
    padded = jnp.pad(cotangent, ((0, 0), (margin, margin), (margin, margin), (0, 0)))
    flipped = jnp.swapaxes(kernel[::-1, ::-1], 2, 3)
    return apply_convolution(padded, flipped, dilation)

def kernel_gradient_fn(padded, cotangent, dilation):
    tile_side = cotangent.shape[1]
    padded_wide = padded.astype(jnp.float32)
    cot_wide = cotangent.astype(jnp.float32)
    rows_out = []
    for tap_row in range(3):
        tap_list = []
        for tap_col in range(3):
            window = padded_wide[:, tap_row * dilation:tap_row * dilation + tile_side, tap_col * dilation:tap_col * dilation + tile_side, :]
            tap_list.append(jnp.einsum('tpqi,tpqo->io', window, cot_wide, precision=lax.Precision.HIGHEST))
        rows_out.append(jnp.stack(tap_list))
    return jnp.stack(rows_out)

def reference(features, cotangent, kernel_first_layer, kernel_second_layer, neighbors, turns):
    gradient_factor = 1.0 / math.sqrt(TILES * SIDE * SIDE)
    kernel_layer_first = kernel_first_layer.astype(jnp.float32)
    kernel_layer_second = kernel_second_layer.astype(jnp.float32)
    bordered_input = margin_everywhere(features, neighbors, turns, FIRST_SPACING)
    preactivation = apply_convolution(bordered_input.astype(jnp.float32), kernel_layer_first, FIRST_SPACING)
    activated, derivative = gelu_pair(preactivation)
    hidden_state = activated.astype(jnp.bfloat16)
    bordered_hidden = margin_everywhere(hidden_state, neighbors, turns, SECOND_SPACING)
    output = apply_convolution(bordered_hidden.astype(jnp.float32), kernel_layer_second, SECOND_SPACING).astype(jnp.bfloat16)
    bordered_hidden_gradient = convolution_backward(cotangent.astype(jnp.float32), kernel_layer_second, SECOND_SPACING).astype(jnp.bfloat16)
    hidden_gradient = margin_transpose(bordered_hidden_gradient.astype(jnp.float32), neighbors, turns, SECOND_SPACING)
    preactivation_gradient = (hidden_gradient * derivative).astype(jnp.bfloat16)
    bordered_input_gradient = convolution_backward(preactivation_gradient.astype(jnp.float32), kernel_layer_first, FIRST_SPACING).astype(jnp.bfloat16)
    features_gradient = margin_transpose(bordered_input_gradient.astype(jnp.float32), neighbors, turns, FIRST_SPACING).astype(jnp.bfloat16)
    second_kernel_gradient = kernel_gradient_fn(bordered_hidden, cotangent, SECOND_SPACING) * gradient_factor
    first_kernel_gradient = kernel_gradient_fn(bordered_input, preactivation_gradient, FIRST_SPACING) * gradient_factor
    return (output, features_gradient, first_kernel_gradient, second_kernel_gradient)
```

```python
import functools
import math

import jax
import jax.numpy as jnp
import numpy as np
from jax import lax
from jax.experimental import pallas as pl
from jax.experimental.pallas import tpu as pltpu
from jax.sharding import PartitionSpec as P

SIDE = 16
PX = SIDE * SIDE
CH = 128
TILES = 128
FIRST, SECOND = 1, 2
SCALE = 1.0 / math.sqrt(TILES * PX)

gelu_scale = 0.7978845608028654
gelu_cubic = 0.044715

F32, BF16 = jnp.float32, jnp.bfloat16
MESH = pl.DeviceIdType.MESH

STRIDE = {"y": 32, "x": 8, "z": 2}
SHIFT = {"y": 5, "x": 3, "z": 1}
PLANS = (("x", "y", "z"), ("y", "z", "x"), ("z", "x", "y"))
LAYER_PLAN = (0, 1, 2, 0, 2, 1)

ROW_STEP = (-1, -1, 0, 1, 1, 1, 0, -1)
COL_STEP = (0, 1, 1, 1, 0, -1, -1, -1)

LAYER_ROWS = 80


def side_pixel(j, depth, along):
    last = SIDE - 1
    return ((depth, along), (along, last - depth), (last - depth, last - along), (last - along, depth))[j]


def layer_rows(width):
    for q in range(5):
        for e in range(4):
            for j in range(4):
                row = q * 16 + e * 4 + j
                if q < 4:
                    yield row, 2 * j, 4 * q + e
                elif 2 - width <= e < 2:
                    yield row, 2 * j + 1, SIDE - 2 + e


def rim_place(d, depth, along, width):
    facing = (d + 4) % 8
    i, j = side_pixel(facing // 2, depth, along)
    return width + SIDE * ROW_STEP[d] + i, width + SIDE * COL_STEP[d] + j


def pick_matrix(depth):
    out = np.zeros((LAYER_ROWS, PX), np.float32)
    for row, compass, along in layer_rows(2):
        i, j = side_pixel(compass // 2, depth, along)
        out[row, i * SIDE + j] = 1
    return out


def shift_matrix(width):
    rows = SIDE + 2 * width
    out = np.zeros((3, rows, SIDE, PX), np.float32)
    for b in range(3):
        for i in range(SIDE):
            for j in range(SIDE):
                src = j + b * width - width
                if 0 <= src < SIDE:
                    out[b, i + width, j, i * SIDE + src] = 1
    return out.reshape(3 * rows * SIDE, PX)


def rim_matrix(width):
    rows = SIDE + 2 * width
    out = np.zeros((3, rows, SIDE, width * LAYER_ROWS), np.float32)
    for depth in range(width):
        for row, d, along in layer_rows(width):
            i, j = rim_place(d, depth, along, width)
            for b in range(3):
                col = j - b * width
                if 0 <= col < SIDE:
                    out[b, i, col, depth * LAYER_ROWS + row] = 1
    return out.reshape(3 * rows * SIDE, width * LAYER_ROWS)


def taps_matrix(width):
    out = np.zeros((3, 3, width * LAYER_ROWS, PX), np.float32)
    for depth in range(width):
        for row, d, along in layer_rows(width):
            i, j = rim_place(d, depth, along, width)
            for a in range(3):
                for b in range(3):
                    si, sj = i - width * (2 - a), j - width * (2 - b)
                    if 0 <= si < SIDE and 0 <= sj < SIDE:
                        out[a, b, depth * LAYER_ROWS + row, si * SIDE + sj] = 1
    return out.reshape(9 * width * LAYER_ROWS, PX)


def constants():
    pick = np.concatenate([pick_matrix(0), pick_matrix(1)])
    arrays = (
        pick,
        np.ascontiguousarray(pick.T),
        shift_matrix(1),
        shift_matrix(2),
        rim_matrix(1),
        rim_matrix(2),
        taps_matrix(1),
        taps_matrix(2),
    )
    return [jnp.asarray(a, BF16) for a in arrays]


def dot(a, b):
    return jnp.dot(a, b, preferred_element_type=F32)


def dot_first(a, b):
    return lax.dot_general(a, b, (((0,), (0,)), ((), ())), preferred_element_type=F32)


def coordinate(index, axis):
    return (index >> SHIFT[axis]) & 3


def block_kernel(
    feat, cot, k1, k2, nb, turns,
    pick, spread, shift1, shift2, rim1, rim2, taps1, taps2,
    out, fgrad, g1_out, g2_out,
    buf, msg, recv, choose, kt1, kt2, x1f, x1g, x2h, x2c, zcat, center, mid, deriv,
    grads, core_in, part, rs_in, z_in, ag_in, sib_in,
    send_sem, recv_sem, ar_send, ar_recv,
):
    me = lax.axis_index("tile")
    core = me & 1
    pos = {axis: coordinate(me, axis) for axis in "yxz"}

    def along(axis, i):
        return me + (((pos[axis] + i) & 3) - pos[axis]) * STRIDE[axis]

    def plane_peers():
        for dy in range(4):
            for dx in range(4):
                if dy or dx:
                    y, x = (pos["y"] + dy) & 3, (pos["x"] + dx) & 3
                    yield me + (y - pos["y"]) * STRIDE["y"] + (x - pos["x"]) * STRIDE["x"], y * 4 + x

    sibling = me + 1 - 2 * core

    peers = [sibling] + [device for device, _ in plane_peers()]
    for axis in "yxz":
        for i in range(1, 4):
            if axis == "z":
                peers.append(along(axis, i))
            peers.append(along(axis, i) + 1 - 2 * core)
    barrier = pltpu.get_barrier_semaphore()
    for device in peers:
        pl.semaphore_signal(barrier, inc=1, device_id=(device,), device_id_type=MESH)

    def remote(src, dst, send, arrive, device):
        pltpu.make_async_remote_copy(
            src_ref=src, dst_ref=dst, send_sem=send, recv_sem=arrive, device_id=(device,), device_id_type=MESH
        ).start()

    def wait_bytes(ref, sem):
        pltpu.make_async_copy(ref, ref, sem).wait()

    def own_rows(layer):
        a, b, _ = PLANS[LAYER_PLAN[layer]]
        return pl.ds(pl.multiple_of((pos[b] * 4 + pos[a]) * 16, 16), 16)

    def put(layer, values):
        buf[layer, :, own_rows(layer), :] = values.astype(BF16).reshape(5, 16, CH)

    def send_a(layer):
        axis = PLANS[LAYER_PLAN[layer]][0]
        view = buf.at[layer, :, own_rows(layer), :]
        for i in range(1, 4):
            remote(view, view, send_sem.at[layer, 0], recv_sem.at[layer, 0], along(axis, i))

    def send_b(layer):
        axis = PLANS[LAYER_PLAN[layer]][1]
        wait_bytes(buf.at[layer, :, pl.ds(0, 48), :], recv_sem.at[layer, 0])
        view = buf.at[layer, :, pl.ds(pl.multiple_of(pos[axis] * 64, 64), 64), :]
        for i in range(1, 4):
            remote(view, view, send_sem.at[layer, 1], recv_sem.at[layer, 1], along(axis, i))

    def send_line(layer, chooser):
        axis = PLANS[LAYER_PLAN[layer]][2]
        wait_bytes(buf.at[layer, :, pl.ds(0, 192), :], recv_sem.at[layer, 1])
        for q in range(5):
            msg[layer, q] = dot(choose[chooser, 0 if q < 4 else 1], buf[layer, q]).astype(BF16)
        mine = pl.ds(pl.multiple_of((pos[axis] * 2 + core) * 16, 16), 16)
        for i in range(4):
            for flip in range(2):
                if i or flip:
                    other = core + flip - 2 * core * flip
                    device = along(axis, i) - core + other
                    theirs = pl.ds(pl.multiple_of((((pos[axis] + i) & 3) * 2 + other) * 16, 16), 16)
                    remote(
                        msg.at[layer, :, theirs, :], recv.at[layer, :, mine, :],
                        send_sem.at[layer, 2], recv_sem.at[layer, 2], device,
                    )
        recv[layer, :, mine, :] = msg[layer, :, mine, :]

    def arrived(layer):
        wait_bytes(recv.at[layer, :, pl.ds(0, 112), :], recv_sem.at[layer, 2])
        total = recv[layer, :, 0:16, :].astype(F32)
        for g in range(1, 8):
            total += recv[layer, :, g * 16 : g * 16 + 16, :].astype(F32)
        return total.reshape(LAYER_ROWS, CH)

    def finish_sends(layer):
        wait_bytes(buf.at[layer, :, pl.ds(0, 48), :], send_sem.at[layer, 0])
        wait_bytes(buf.at[layer, :, pl.ds(0, 192), :], send_sem.at[layer, 1])
        wait_bytes(recv.at[layer, :, pl.ds(0, 112), :], send_sem.at[layer, 2])

    def table_rows(device_of_row, column_of_row):
        rows = device_of_row.shape[0]
        ids = lax.broadcasted_iota(jnp.int32, (rows, TILES), 1)
        hot = jnp.where(ids == device_of_row, 1.0, 0.0).astype(BF16)
        keep = lax.broadcasted_iota(jnp.int32, (rows, 8), 1) == column_of_row
        picked = []
        for table in (nb, turns):
            values = dot(hot, table[...].astype(F32).astype(BF16))
            values = jnp.sum(jnp.where(keep, values, 0.0), axis=1, keepdims=True)
            picked.append(values.astype(jnp.int32))
        return picked

    def build_forward(slot, plan):
        a, b, line = PLANS[plan]
        row = lax.broadcasted_iota(jnp.int32, (128, 1), 0)
        dest = me - core - pos[line] * STRIDE[line] + (row >> 5) * STRIDE[line] + ((row >> 4) & 1)
        e, j = (row >> 2) & 3, row & 3
        for corner in range(2):
            source, quarter = table_rows(dest, 2 * j + corner)
            here = (source >= 0) & (coordinate(source, line) == pos[line]) & ((source & 1) == core)
            place = (coordinate(source, b) * 4 + coordinate(source, a)) * 16 + e * 4 + ((j + 2 + quarter) & 3)
            place = jnp.where(here, place, -1)
            lanes = lax.broadcasted_iota(jnp.int32, (128, PX), 1)
            choose[slot, corner] = jnp.where(lanes == place, 1.0, 0.0).astype(BF16)

    def build_adjoint(slot, plan):
        a, b, line = PLANS[plan]
        row = lax.broadcasted_iota(jnp.int32, (PX, 1), 0)
        owner = (
            me - pos[a] * STRIDE[a] - pos[b] * STRIDE[b]
            + (row >> 6) * STRIDE[b] + ((row >> 4) & 3) * STRIDE[a]
        )
        e, j = (row >> 2) & 3, row & 3
        for corner in range(2):
            target, quarter = table_rows(owner, 2 * j + corner)
            here = (target >= 0) & (coordinate(target, a) == pos[a]) & (coordinate(target, b) == pos[b])
            place = (coordinate(target, line) * 2 + (target & 1)) * 16 + e * 4 + ((j + 2 + quarter) & 3)
            place = jnp.where(here, place, -1)
            lanes = lax.broadcasted_iota(jnp.int32, (PX, 128), 1)
            choose[slot, corner] = jnp.where(lanes == place, 1.0, 0.0).T.astype(BF16)

    def flip_kernel(kernel, dest):
        for a in range(3):
            for b in range(3):
                tap = kernel[2 - a, (2 - b) * CH : (3 - b) * CH, :]
                at = (a * 3 + b) * CH
                dest[at : at + CH, :] = tap.astype(F32).T.astype(BF16)

    def lay(dest, columns):
        rows = dest.shape[0]
        for b in range(3):
            dest[:, b * CH : (b + 1) * CH] = columns[b * rows : (b + 1) * rows].astype(BF16)

    def conv(x, kernel, dilation):
        total = None
        for a in range(3):
            window = x[a * dilation * SIDE : a * dilation * SIDE + PX, :]
            tap = dot(window, kernel(a))
            total = tap if total is None else total + tap
        return total

    def rim_gradient(values, taps, kernel_t, width):
        rows = width * LAYER_ROWS
        for tap in range(9):
            shifted = dot(taps[tap * rows : (tap + 1) * rows, :], values)
            zcat[0:rows, tap * CH : (tap + 1) * CH] = shifted.astype(BF16)
        return dot(zcat[0:rows, :], kernel_t[...])

    def kernel_gradient(which, x, right, dilation):
        for a in range(3):
            window = x[a * dilation * SIDE : a * dilation * SIDE + PX, :]
            grads[which, a * 3 * CH : (a + 1) * 3 * CH, :] = dot_first(window, right)

    half = pl.multiple_of(core * 32, 8)
    other_half = pl.multiple_of(32 - core * 32, 8)
    owner = pos["y"] * 4 + pos["x"]

    def ar_core(which):
        for i in range(16):
            remote(
                grads.at[which, pl.ds(pl.multiple_of(i * 72 + other_half, 8), 40), :], core_in.at[which, i],
                ar_send.at[which, 0], ar_recv.at[which, 0], sibling,
            )

    def ar_scatter(which):
        wait_bytes(core_in.at[which], ar_recv.at[which, 0])
        for i in range(16):
            mine = grads[which, pl.ds(pl.multiple_of(i * 72 + half, 8), 40), :]
            part[which, i] = mine + core_in[which, i]
        for device, i in plane_peers():
            remote(part.at[which, i], rs_in.at[which, owner], ar_send.at[which, 1], ar_recv.at[which, 1], device)
        rs_in[which, owner] = part[which, owner]

    def ar_line(which):
        wait_bytes(rs_in.at[which, pl.ds(0, 15)], ar_recv.at[which, 1])
        total = rs_in[which, 0]
        for i in range(1, 16):
            total += rs_in[which, i]
        z_in[which, pos["z"]] = total
        for i in range(1, 4):
            remote(
                z_in.at[which, pos["z"]], z_in.at[which, pos["z"]],
                ar_send.at[which, 2], ar_recv.at[which, 2], along("z", i),
            )

    def ar_gather(which):
        wait_bytes(z_in.at[which, pl.ds(0, 3)], ar_recv.at[which, 2])
        total = ((z_in[which, 0] + z_in[which, 1]) + z_in[which, 2]) + z_in[which, 3]
        ag_in[which, owner] = total * SCALE
        for device, _ in plane_peers():
            remote(
                ag_in.at[which, owner], ag_in.at[which, owner],
                ar_send.at[which, 3], ar_recv.at[which, 3], device,
            )

    def ar_share(which):
        wait_bytes(ag_in.at[which, pl.ds(0, 15)], ar_recv.at[which, 3])
        remote(ag_in.at[which], sib_in.at[which], ar_send.at[which, 4], ar_recv.at[which, 4], sibling)

    def ar_finish(which, dest):
        wait_bytes(sib_in.at[which], ar_recv.at[which, 4])
        first = core == 0
        for i in range(16):
            mine, theirs = ag_in[which, i], sib_in[which, i]
            dest[i * 72 : i * 72 + 40, :] = jnp.where(first, mine, theirs)
            dest[i * 72 + 40 : i * 72 + 72, :] = jnp.where(first, theirs, mine)[8:40]
        wait_bytes(core_in.at[which], ar_send.at[which, 0])
        wait_bytes(rs_in.at[which, pl.ds(0, 15)], ar_send.at[which, 1])
        wait_bytes(z_in.at[which, pl.ds(0, 3)], ar_send.at[which, 2])
        wait_bytes(ag_in.at[which, pl.ds(0, 15)], ar_send.at[which, 3])
        wait_bytes(sib_in.at[which], ar_send.at[which, 4])

    put(0, dot(pick[0:LAYER_ROWS, :], feat[...]))
    flip_kernel(k2, kt2)
    rim = rim_gradient(cot[...], taps2, kt2, SECOND)
    put(1, rim[0:LAYER_ROWS])
    put(2, rim[LAYER_ROWS : 2 * LAYER_ROWS])
    pl.semaphore_wait(barrier, len(peers))
    for layer in range(3):
        send_a(layer)
    build_forward(0, 0)
    build_adjoint(1, 1)
    build_adjoint(2, 2)
    for layer in range(3):
        send_b(layer)
    center[0 : 3 * 288, :] = dot(shift1[...], feat[...])
    lay(x2c, dot(shift2[...], cot[...]))
    mid[...] = conv(x2c, lambda a: kt2[a * 384 : (a + 1) * 384, :], SECOND).astype(BF16)
    for layer in range(3):
        send_line(layer, layer)
    flip_kernel(k1, kt1)
    build_forward(3, 2)

    lay(x1f, center[0 : 3 * 288, :] + dot(rim1[...], arrived(0).astype(BF16)))
    v = conv(x1f, lambda a: k1[a], FIRST)
    tangent = jnp.tanh(gelu_scale * (v + gelu_cubic * v * v * v))
    hidden = (0.5 * v * (1.0 + tangent)).astype(BF16)
    deriv[...] = 0.5 * (1.0 + tangent) + 0.5 * v * (1.0 - tangent * tangent) * gelu_scale * (
        1.0 + 3.0 * gelu_cubic * v * v
    )
    rows = dot(pick[...], hidden)
    put(3, rows[0:LAYER_ROWS])
    put(4, rows[LAYER_ROWS : 2 * LAYER_ROWS])
    send_a(3)
    send_a(4)

    sums = jnp.concatenate([arrived(1), arrived(2)], axis=0)
    high = sums.astype(BF16)
    low = (sums - high.astype(F32)).astype(BF16)
    grad_hidden = mid[...].astype(F32) + dot(spread[...], high) + dot(spread[...], low)
    gpre = (grad_hidden * deriv[...]).astype(BF16)
    put(5, rim_gradient(gpre, taps1, kt1, FIRST))
    send_a(5)
    kernel_gradient(0, x1f, gpre, FIRST)
    ar_core(0)
    send_b(3)
    send_b(4)
    center[...] = dot(shift2[...], hidden)
    send_b(5)
    lay(x1g, dot(shift1[...], gpre))
    mid[...] = conv(x1g, lambda a: kt1[a * 384 : (a + 1) * 384, :], FIRST).astype(BF16)
    ar_scatter(0)
    send_line(3, 0)
    send_line(4, 3)
    send_line(5, 1)
    ar_line(0)

    rims = jnp.concatenate([arrived(3), arrived(4)], axis=0).astype(BF16)
    lay(x2h, center[...] + dot(rim2[...], rims))
    kernel_gradient(1, x2h, cot[...], SECOND)
    ar_core(1)
    out[...] = conv(x2h, lambda a: k2[a], SECOND).astype(BF16)
    ar_gather(0)
    ar_scatter(1)
    sums = arrived(5)
    high = sums.astype(BF16)
    low = (sums - high.astype(F32)).astype(BF16)
    fgrad[...] = (
        mid[...].astype(F32) + dot(spread[:, 0:LAYER_ROWS], high) + dot(spread[:, 0:LAYER_ROWS], low)
    ).astype(BF16)
    ar_share(0)
    ar_line(1)
    ar_finish(0, g1_out)
    ar_gather(1)
    for layer in range(6):
        finish_sends(layer)
    ar_share(1)
    ar_finish(1, g2_out)


def local(features, cotangent, kernel_first_layer, kernel_second_layer, neighbors, turns):
    vmem = pl.BlockSpec(memory_space=pltpu.VMEM)
    operands = [
        features.reshape(PX, CH),
        cotangent.reshape(PX, CH),
        kernel_first_layer.reshape(3, 3 * CH, CH),
        kernel_second_layer.reshape(3, 3 * CH, CH),
        neighbors,
        turns,
    ] + constants()
    output, features_gradient, first, second = pl.pallas_call(
        block_kernel,
        out_shape=(
            jax.ShapeDtypeStruct((PX, CH), BF16),
            jax.ShapeDtypeStruct((PX, CH), BF16),
            jax.ShapeDtypeStruct((9 * CH, CH), F32),
            jax.ShapeDtypeStruct((9 * CH, CH), F32),
        ),
        in_specs=[vmem] * len(operands),
        out_specs=(vmem,) * 4,
        scratch_shapes=[
            pltpu.VMEM((6, 5, 256, CH), BF16),
            pltpu.VMEM((6, 5, 128, CH), BF16),
            pltpu.VMEM((6, 5, 128, CH), BF16),
            pltpu.VMEM((4, 2, 128, PX), BF16),
            pltpu.VMEM((9 * CH, CH), BF16),
            pltpu.VMEM((9 * CH, CH), BF16),
            pltpu.VMEM((288, 3 * CH), BF16),
            pltpu.VMEM((288, 3 * CH), BF16),
            pltpu.VMEM((320, 3 * CH), BF16),
            pltpu.VMEM((320, 3 * CH), BF16),
            pltpu.VMEM((2 * LAYER_ROWS, 9 * CH), BF16),
            pltpu.VMEM((3 * 320, CH), F32),
            pltpu.VMEM((PX, CH), BF16),
            pltpu.VMEM((PX, CH), F32),
            pltpu.VMEM((2, 9 * CH, CH), F32),
            pltpu.VMEM((2, 16, 40, CH), F32),
            pltpu.VMEM((2, 16, 40, CH), F32),
            pltpu.VMEM((2, 16, 40, CH), F32),
            pltpu.VMEM((2, 4, 40, CH), F32),
            pltpu.VMEM((2, 16, 40, CH), F32),
            pltpu.VMEM((2, 16, 40, CH), F32),
            pltpu.SemaphoreType.DMA((6, 3)),
            pltpu.SemaphoreType.DMA((6, 3)),
            pltpu.SemaphoreType.DMA((2, 5)),
            pltpu.SemaphoreType.DMA((2, 5)),
        ],
        compiler_params=pltpu.CompilerParams(
            collective_id=0, has_side_effects=True, vmem_limit_bytes=48 * 2**20
        ),
    )(*operands)
    return (
        output.reshape(features.shape),
        features_gradient.reshape(features.shape),
        first.reshape(kernel_first_layer.shape),
        second.reshape(kernel_second_layer.shape),
    )


def solution(mesh):
    placed = (P("tile", None, None, None), P("tile", None, None, None), P(), P(), P(), P())
    return jax.shard_map(
        local,
        mesh=mesh,
        in_specs=placed,
        out_specs=(P("tile", None, None, None), P("tile", None, None, None), P(), P()),
        check_vma=False,
    )
```

```python
import functools
import math

import jax
import jax.numpy as jnp
import numpy as np
from jax import lax
from jax.experimental import pallas as pl
from jax.experimental.pallas import tpu as pltpu
from jax.sharding import PartitionSpec as P

SIDE = 16
PX = SIDE * SIDE
CH = 128
TILES = 128
FIRST, SECOND = 1, 2
SCALE = 1.0 / math.sqrt(TILES * PX)

gelu_scale = 0.7978845608028654
gelu_cubic = 0.044715

F32, BF16 = jnp.float32, jnp.bfloat16
MESH = pl.DeviceIdType.MESH

STRIDE = {"y": 32, "x": 8, "z": 2}
SHIFT = {"y": 5, "x": 3, "z": 1}
PLANS = (("x", "y", "z"), ("y", "z", "x"), ("z", "x", "y"))
LAYER_PLAN = (0, 1, 2, 0, 2, 1)
LAYERS = 6
SLICES = (4, 4, 4, 4, 4, 5)
CORNER_SLICE = (3, 0, 0, 3, 3, 4)

ROW_STEP = (-1, -1, 0, 1, 1, 1, 0, -1)
COL_STEP = (0, 1, 1, 1, 0, -1, -1, -1)

LAYER_ROWS = 80

FAR_FIRST = (2, 1, 3)

CHUNK, HALF = 72, 48
SUM_PLANS = (("z", "x", "y"), ("x", "y", "z"))


def side_pixel(j, depth, along):
    last = SIDE - 1
    return ((depth, along), (along, last - depth), (last - depth, last - along), (last - along, depth))[j]


def layer_rows(width):
    for q in range(5):
        for e in range(4):
            for j in range(4):
                row = q * 16 + e * 4 + j
                if q < 4:
                    yield row, 2 * j, 4 * q + e
                elif 2 - width <= e < 2:
                    yield row, 2 * j + 1, SIDE - 2 + e


def rim_place(d, depth, along, width):
    facing = (d + 4) % 8
    i, j = side_pixel(facing // 2, depth, along)
    return width + SIDE * ROW_STEP[d] + i, width + SIDE * COL_STEP[d] + j


def pick_matrix(depth):
    out = np.zeros((LAYER_ROWS, PX), np.float32)
    for row, compass, along in layer_rows(2):
        i, j = side_pixel(compass // 2, depth, along)
        out[row, i * SIDE + j] = 1
    return out


def shift_matrix(width):
    rows = SIDE + 2 * width
    out = np.zeros((3, rows, SIDE, PX), np.float32)
    for b in range(3):
        for i in range(SIDE):
            for j in range(SIDE):
                src = j + b * width - width
                if 0 <= src < SIDE:
                    out[b, i + width, j, i * SIDE + src] = 1
    return out.reshape(3 * rows * SIDE, PX)


def rim_matrix(width):
    rows = SIDE + 2 * width
    out = np.zeros((3, rows, SIDE, width * LAYER_ROWS), np.float32)
    for depth in range(width):
        for row, d, along in layer_rows(width):
            i, j = rim_place(d, depth, along, width)
            for b in range(3):
                col = j - b * width
                if 0 <= col < SIDE:
                    out[b, i, col, depth * LAYER_ROWS + row] = 1
    return out.reshape(3 * rows * SIDE, width * LAYER_ROWS)


def taps_matrix(width):
    out = np.zeros((3, 3, width * LAYER_ROWS, PX), np.float32)
    for depth in range(width):
        for row, d, along in layer_rows(width):
            i, j = rim_place(d, depth, along, width)
            for a in range(3):
                for b in range(3):
                    si, sj = i - width * (2 - a), j - width * (2 - b)
                    if 0 <= si < SIDE and 0 <= sj < SIDE:
                        out[a, b, depth * LAYER_ROWS + row, si * SIDE + sj] = 1
    return out.reshape(9 * width * LAYER_ROWS, PX)


SIDE_TAP = ((0, 1), (1, 2), (2, 1), (1, 0))
CORNER_TAP = ((0, 2), (2, 2), (2, 0), (0, 0))
SLIDES = (-2, 0, 2)


def met_pixel(d, depth, along, tap):
    i, j = rim_place(d, depth, along, 2)
    return i - 2 * tap[0], j - 2 * tap[1]


def met_matrix():
    out = np.zeros((2, LAYER_ROWS, PX), np.float32)
    for depth in range(2):
        for row, d, along in layer_rows(2):
            i, j = met_pixel(d, depth, along, CORNER_TAP[d // 2] if d % 2 else SIDE_TAP[d // 2])
            out[depth, row, i * SIDE + j] = 1
    return out.reshape(2 * LAYER_ROWS, PX)


def slide_tap(j, slide):
    target = met_pixel(2 * j, 0, 7 + slide, SIDE_TAP[j])
    return [(a, b) for a in range(3) for b in range(3) if met_pixel(2 * j, 0, 7, (a, b)) == target][0]


def constants():
    pick = np.concatenate([pick_matrix(0), pick_matrix(1)])
    arrays = (
        pick,
        np.ascontiguousarray(pick.T),
        shift_matrix(1),
        shift_matrix(2),
        rim_matrix(1),
        rim_matrix(2),
        taps_matrix(1),
        met_matrix(),
    )
    return [jnp.asarray(a, BF16) for a in arrays]


def dot(a, b):
    return jnp.dot(a, b, preferred_element_type=F32)


def dot_first(a, b):
    return lax.dot_general(a, b, (((0,), (0,)), ((), ())), preferred_element_type=F32)


def coordinate(index, axis):
    return (index >> SHIFT[axis]) & 3


def block_kernel(
    feat_in, cot_in, k1_in, k2_in, nb_in, turns_in,
    pick_in, spread_in, shift1_in, shift2_in, rim1_in, rim2_in, taps1_in, met_in,
    out_hbm, fgrad_hbm, halves_hbm,
    feat, cot, k1, k2, nb, turns, pick, spread, shift1, shift2, rim1, rim2, taps1, met,
    buf, msg, recv, choose, kt1, kt2, x1f, x1g, x2h, x2c, zcat, center, mid, deriv,
    strip, strip_in, slid, met_side, met_corner, tap_kernels,
    grads, core_in, part, rs_in, line_in, ag_in, out, fgrad,
    send_sem, recv_sem, ar_send, ar_recv, load_sem, store_sem, strip_sem, go_sem,
):
    me = lax.axis_index("tile")
    core = me & 1
    pos = {axis: coordinate(me, axis) for axis in "yxz"}

    def along(axis, i):
        return me + (((pos[axis] + i) & 3) - pos[axis]) * STRIDE[axis]

    def plane_peers(a, b):
        steps = [(da, db) for da in range(4) for db in range(4) if da or db]
        for da, db in sorted(steps, key=lambda step: -sum(min(d, 4 - d) for d in step)):
            at_a, at_b = (pos[a] + da) & 3, (pos[b] + db) & 3
            yield me + (at_a - pos[a]) * STRIDE[a] + (at_b - pos[b]) * STRIDE[b], at_b * 4 + at_a

    sibling = me + 1 - 2 * core

    peers = [sibling] + [along(axis, i) for axis in "xyz" for i in FAR_FIRST]
    barrier = pltpu.get_barrier_semaphore()
    for device in peers:
        pl.semaphore_signal(barrier, inc=1, device_id=(device,), device_id_type=MESH)

    loads = {}
    for i, (name, src, dst) in enumerate(
        (
            ("pick", pick_in, pick), ("feat", feat_in, feat), ("met", met_in, met), ("cot", cot_in, cot),
            ("k2", k2_in, k2), ("nb", nb_in, nb), ("turns", turns_in, turns),
            ("shift1", shift1_in, shift1), ("shift2", shift2_in, shift2), ("rim1", rim1_in, rim1),
            ("k1", k1_in, k1), ("spread", spread_in, spread), ("taps1", taps1_in, taps1), ("rim2", rim2_in, rim2),
        )
    ):
        loads[name] = pltpu.make_async_copy(src, dst, load_sem.at[i])
        loads[name].start()

    def loaded(*names):
        for name in names:
            loads[name].wait()

    def remote(src, dst, send, arrive, device):
        pltpu.make_async_remote_copy(
            src_ref=src, dst_ref=dst, send_sem=send, recv_sem=arrive, device_id=(device,), device_id_type=MESH
        ).start()

    def wait_bytes(ref, sem):
        pltpu.make_async_copy(ref, ref, sem).wait()

    def own_rows(layer):
        a, b, _ = PLANS[LAYER_PLAN[layer]]
        return pl.ds(pl.multiple_of((pos[b] * 4 + pos[a]) * 16, 16), 16)

    def put(layer, values):
        n = SLICES[layer]
        buf[layer, 0:n, own_rows(layer), :] = values[0 : n * 16].astype(BF16).reshape(n, 16, CH)

    def blocks(layer, count):
        return buf.at[layer, pl.ds(0, SLICES[layer]), pl.ds(0, count * 16), :]

    def send_a(layer):
        axis = PLANS[LAYER_PLAN[layer]][0]
        view = buf.at[layer, pl.ds(0, SLICES[layer]), own_rows(layer), :]
        for i in FAR_FIRST:
            remote(view, view, send_sem.at[layer, 0], recv_sem.at[layer, 0], along(axis, i))

    def gathered(layer):
        wait_bytes(blocks(layer, 12), recv_sem.at[layer, 1])

    def send_b(layer):
        axis = PLANS[LAYER_PLAN[layer]][1]
        wait_bytes(blocks(layer, 3), recv_sem.at[layer, 0])
        view = buf.at[layer, pl.ds(0, SLICES[layer]), pl.ds(pl.multiple_of(pos[axis] * 64, 64), 64), :]
        for i in FAR_FIRST:
            remote(view, view, send_sem.at[layer, 1], recv_sem.at[layer, 1], along(axis, i))

    def send_line(layer, chooser):
        gathered(layer)
        for q in range(5):
            source = buf[layer, q if q < 4 else CORNER_SLICE[layer]]
            msg[layer, q] = dot(choose[chooser, 0 if q < 4 else 1], source).astype(BF16)
        deliver(layer)

    def deliver(layer):
        axis = PLANS[LAYER_PLAN[layer]][2]
        mine = pl.ds(pl.multiple_of((pos[axis] * 2 + core) * 16, 16), 16)
        for i in FAR_FIRST + (0,):
            for flip in range(2):
                if i or flip:
                    other = core + flip - 2 * core * flip
                    device = along(axis, i) - core + other
                    theirs = pl.ds(pl.multiple_of((((pos[axis] + i) & 3) * 2 + other) * 16, 16), 16)
                    remote(
                        msg.at[layer, :, theirs, :], recv.at[layer, :, mine, :],
                        send_sem.at[layer, 2], recv_sem.at[layer, 2], device,
                    )
        recv[layer, :, mine, :] = msg[layer, :, mine, :]

    def send_strip(depth, values):
        axis = PLANS[LAYER_PLAN[1 + depth]][2]
        strip[depth] = values.astype(BF16).reshape(5, 16, CH)
        mine = pl.ds(pl.multiple_of((pos[axis] * 2 + core) * 16, 16), 16)
        for i in FAR_FIRST + (0,):
            for flip in range(2):
                if i or flip:
                    device = along(axis, i) + flip - 2 * core * flip
                    remote(
                        strip.at[depth], strip_in.at[depth, :, mine, :],
                        strip_sem.at[0, depth], strip_sem.at[1, depth], device,
                    )
        strip_in[depth, :, mine, :] = strip[depth]

    def meet(layer):
        gathered(layer)
        depth = layer - 1
        lane = lax.broadcasted_iota(jnp.int32, (128, PX), 1) & 3
        for corner in range(2):
            full = choose[layer, corner].astype(F32)
            split = jnp.concatenate([jnp.where(lane == j, full, 0.0).astype(BF16) for j in range(4)], axis=0)
            for q in (4,) if corner else range(4):
                found = dot(split, buf[layer, q if q < 4 else CORNER_SLICE[layer]]).astype(BF16)
                for j in range(4):
                    part_j = found[j * 128 : (j + 1) * 128]
                    if corner:
                        met_corner[depth * 128 : (depth + 1) * 128, j * CH : (j + 1) * CH] = part_j
                    else:
                        at = (depth * 4 + q) * 128
                        met_side[at : at + 128, j * CH : (j + 1) * CH] = part_j

    def slide(x, step):
        x = x.reshape(4, 8, 2, 8, CH)
        empty = jnp.zeros((1, 8, 1, 8, CH), F32)
        first, second = x[:, :, 0:1], x[:, :, 1:2]
        if step < 0:
            x = jnp.concatenate([jnp.concatenate([empty, second[0:3]], axis=0), first], axis=2)
        elif step > 0:
            x = jnp.concatenate([second, jnp.concatenate([first[1:4], empty], axis=0)], axis=2)
        return x.reshape(512, CH)

    def send_rim_gradient(layer):
        depth = layer - 1
        meet(layer)
        terms = dot(met_side[depth * 512 : (depth + 1) * 512, :], tap_kernels[:, 0 : 3 * CH])
        total = None
        for k, step in enumerate(SLIDES):
            term = slide(terms[:, k * CH : (k + 1) * CH], step)
            total = term if total is None else total + term
        msg[layer, 0:4] = total.astype(BF16).reshape(4, 128, CH)
        corner = dot(met_corner[depth * 128 : (depth + 1) * 128, :], tap_kernels[:, 3 * CH : 4 * CH])
        msg[layer, 4] = corner.astype(BF16)
        deliver(layer)

    def lay_taps():
        for j in range(4):
            taps = [slide_tap(j, step) for step in SLIDES] + [CORNER_TAP[j]]
            for k, (a, b) in enumerate(taps):
                at = ((2 - a) * 3 + 2 - b) * CH
                tap_kernels[j * CH : (j + 1) * CH, k * CH : (k + 1) * CH] = kt2[at : at + CH, :]

    def slide_strips(depth):
        wait_bytes(strip_in.at[depth, :, pl.ds(0, 112), :], strip_sem.at[1, depth])
        x = strip_in[depth, 0:4].astype(F32)
        for k, step in enumerate(SLIDES):
            slid[depth * 512 : (depth + 1) * 512, k * CH : (k + 1) * CH] = slide(x, -step).astype(BF16)

    def arrived(layer):
        wait_bytes(recv.at[layer, :, pl.ds(0, 112), :], recv_sem.at[layer, 2])
        total = recv[layer, :, 0:16, :].astype(F32)
        for g in range(1, 8):
            total += recv[layer, :, g * 16 : g * 16 + 16, :].astype(F32)
        return total.reshape(LAYER_ROWS, CH)

    def finish_sends(layer):
        wait_bytes(blocks(layer, 3), send_sem.at[layer, 0])
        wait_bytes(blocks(layer, 12), send_sem.at[layer, 1])
        wait_bytes(recv.at[layer, :, pl.ds(0, 112), :], send_sem.at[layer, 2])

    def table_rows(device_of_row, column_of_row):
        rows = device_of_row.shape[0]
        ids = lax.broadcasted_iota(jnp.int32, (rows, TILES), 1)
        hot = jnp.where(ids == device_of_row, 1.0, 0.0).astype(BF16)
        keep = lax.broadcasted_iota(jnp.int32, (rows, 8), 1) == column_of_row
        picked = []
        for table in (nb, turns):
            values = lax.dot_general(
                hot, table[...].astype(F32).astype(BF16), (((1,), (1,)), ((), ())), preferred_element_type=F32
            )
            values = jnp.sum(jnp.where(keep, values, 0.0), axis=1, keepdims=True)
            picked.append(values.astype(jnp.int32))
        return picked

    def build_forward(slot, plan):
        a, b, line = PLANS[plan]
        row = lax.broadcasted_iota(jnp.int32, (128, 1), 0)
        dest = me - core - pos[line] * STRIDE[line] + (row >> 5) * STRIDE[line] + ((row >> 4) & 1)
        e, j = (row >> 2) & 3, row & 3
        for corner in range(2):
            source, quarter = table_rows(dest, 2 * j + corner)
            here = (source >= 0) & (coordinate(source, line) == pos[line]) & ((source & 1) == core)
            place = (coordinate(source, b) * 4 + coordinate(source, a)) * 16 + e * 4 + ((j + 2 + quarter) & 3)
            if corner:
                here, place = here & (e < 2), place + 8
            place = jnp.where(here, place, -1)
            lanes = lax.broadcasted_iota(jnp.int32, (128, PX), 1)
            choose[slot, corner] = jnp.where(lanes == place, 1.0, 0.0).astype(BF16)

    def build_adjoint(slot, plan):
        a, b, line = PLANS[plan]
        row = lax.broadcasted_iota(jnp.int32, (PX, 1), 0)
        owner = (
            me - pos[a] * STRIDE[a] - pos[b] * STRIDE[b]
            + (row >> 6) * STRIDE[b] + ((row >> 4) & 3) * STRIDE[a]
        )
        e, j = (row >> 2) & 3, row & 3
        for corner in range(2):
            target, quarter = table_rows(owner, 2 * j + corner)
            here = (target >= 0) & (coordinate(target, a) == pos[a]) & (coordinate(target, b) == pos[b])
            place = (coordinate(target, line) * 2 + (target & 1)) * 16 + e * 4 + ((j + 2 + quarter) & 3)
            place = jnp.where(here, place, -1)
            lanes = lax.broadcasted_iota(jnp.int32, (PX, 128), 1)
            choose[slot, corner] = jnp.where(lanes == place, 1.0, 0.0).T.astype(BF16)

    def flip_kernel(kernel, dest):
        for a in range(3):
            for b in range(3):
                tap = kernel[2 - a, (2 - b) * CH : (3 - b) * CH, :]
                at = (a * 3 + b) * CH
                dest[at : at + CH, :] = tap.astype(F32).T.astype(BF16)

    def lay(dest, columns):
        rows = dest.shape[0]
        for b in range(3):
            dest[:, b * CH : (b + 1) * CH] = columns[b * rows : (b + 1) * rows].astype(BF16)

    def conv(x, kernel, dilation):
        total = None
        for a in range(3):
            window = x[a * dilation * SIDE : a * dilation * SIDE + PX, :]
            tap = dot(window, kernel(a))
            total = tap if total is None else total + tap
        return total

    def rim_gradient(values, taps, kernel_t, width):
        rows = width * LAYER_ROWS
        for tap in range(9):
            shifted = dot(taps[tap * rows : (tap + 1) * rows, :], values)
            zcat[0:rows, tap * CH : (tap + 1) * CH] = shifted.astype(BF16)
        return dot(zcat[0:rows, :], kernel_t[...])

    def put_rows(which, start, values, add=False):
        at = 0
        while at < values.shape[0]:
            i, row = divmod(start + at, CHUNK)
            size = min(CHUNK - row, values.shape[0] - at)
            piece = values[at : at + size]
            if add:
                piece = piece + grads[which, i, row : row + size, :]
            grads[which, i, row : row + size, :] = piece
            at += size

    def kernel_gradient(which, x, right, dilation):
        for a in range(3):
            window = x[a * dilation * SIDE : a * dilation * SIDE + PX, :]
            put_rows(which, a * 3 * CH, dot_first(window, right))

    half = pl.multiple_of(core * (CHUNK - HALF), 8)
    other_half = pl.multiple_of((1 - core) * (CHUNK - HALF), 8)
    owners = [pos[b] * 4 + pos[a] for a, b, _ in SUM_PLANS]

    def ar_core(which):
        remote(
            grads.at[which, :, pl.ds(other_half, HALF), :], core_in.at[which],
            ar_send.at[which, 0], ar_recv.at[which, 0], sibling,
        )

    def ar_scatter(which):
        wait_bytes(core_in.at[which], ar_recv.at[which, 0])
        part[which] = (grads[which, :, pl.ds(half, HALF), :] + core_in[which]).astype(BF16)
        for device, i in plane_peers(*SUM_PLANS[which][:2]):
            remote(
                part.at[which, i], rs_in.at[which, owners[which]],
                ar_send.at[which, 1], ar_recv.at[which, 1], device,
            )
        rs_in[which, owners[which]] = part[which, owners[which]]

    def ar_line(which):
        axis = SUM_PLANS[which][2]
        wait_bytes(rs_in.at[which, pl.ds(0, 15)], ar_recv.at[which, 1])
        total = rs_in[which, 0].astype(F32)
        for i in range(1, 16):
            total += rs_in[which, i].astype(F32)
        line_in[which, pos[axis]] = total
        for i in FAR_FIRST:
            remote(
                line_in.at[which, pos[axis]], line_in.at[which, pos[axis]],
                ar_send.at[which, 2], ar_recv.at[which, 2], along(axis, i),
            )

    def ar_gather(which):
        wait_bytes(line_in.at[which, pl.ds(0, 3)], ar_recv.at[which, 2])
        total = ((line_in[which, 0] + line_in[which, 1]) + line_in[which, 2]) + line_in[which, 3]
        ag_in[which, owners[which]] = (total * SCALE).astype(BF16)
        for device, _ in plane_peers(*SUM_PLANS[which][:2]):
            remote(
                ag_in.at[which, owners[which]], ag_in.at[which, owners[which]],
                ar_send.at[which, 3], ar_recv.at[which, 3], device,
            )

    def ar_share(which):
        wait_bytes(ag_in.at[which, pl.ds(0, 15)], ar_recv.at[which, 3])
        remote(ag_in.at[which], halves_hbm.at[which, core], ar_send.at[which, 4], ar_recv.at[which, 4], sibling)
        pltpu.make_async_copy(ag_in.at[which], halves_hbm.at[which, core], store_sem.at[which]).start()

    def ar_finish(which):
        wait_bytes(ag_in.at[which], ar_recv.at[which, 4])
        pltpu.make_async_copy(ag_in.at[which], halves_hbm.at[which, core], store_sem.at[which]).wait()

    def ar_sent(which):
        wait_bytes(core_in.at[which], ar_send.at[which, 0])
        wait_bytes(rs_in.at[which, pl.ds(0, 15)], ar_send.at[which, 1])
        wait_bytes(line_in.at[which, pl.ds(0, 3)], ar_send.at[which, 2])
        wait_bytes(ag_in.at[which, pl.ds(0, 15)], ar_send.at[which, 3])
        wait_bytes(ag_in.at[which], ar_send.at[which, 4])

    loaded("pick", "feat")
    put(0, dot(pick[0:LAYER_ROWS, :], feat[...]))
    loaded("met", "cot")
    rows = dot(met[...], cot[...])
    put(1, rows[0:LAYER_ROWS])
    put(2, rows[LAYER_ROWS : 2 * LAYER_ROWS])
    pl.semaphore_wait(barrier, len(peers))
    pl.semaphore_signal(go_sem, inc=1, device_id=(sibling,), device_id_type=MESH)
    for layer in range(3):
        send_a(layer)
    loaded("nb", "turns", "shift1", "shift2")
    build_forward(0, 0)
    build_adjoint(1, 1)
    build_adjoint(2, 2)
    for layer in range(3):
        send_b(layer)
    loaded("k2")
    flip_kernel(k2, kt2)
    lay_taps()
    center[0 : 3 * 288, :] = dot(shift1[...], feat[...])
    lay(x2c, dot(shift2[...], cot[...]))
    mid[...] = conv(x2c, lambda a: kt2[a * 384 : (a + 1) * 384, :], SECOND).astype(BF16)
    loaded("k1", "rim1", "spread", "taps1", "rim2")
    flip_kernel(k1, kt1)
    build_forward(3, 2)
    pl.semaphore_wait(go_sem, 1)
    send_line(0, 0)
    send_rim_gradient(1)
    send_rim_gradient(2)

    lay(x1f, center[0 : 3 * 288, :] + dot(rim1[...], arrived(0).astype(BF16)))
    v = conv(x1f, lambda a: k1[a], FIRST)
    tangent = jnp.tanh(gelu_scale * (v + gelu_cubic * v * v * v))
    hidden = (0.5 * v * (1.0 + tangent)).astype(BF16)
    deriv[...] = 0.5 * (1.0 + tangent) + 0.5 * v * (1.0 - tangent * tangent) * gelu_scale * (
        1.0 + 3.0 * gelu_cubic * v * v
    )
    rows = dot(pick[...], hidden)
    put(3, rows[0:LAYER_ROWS])
    put(4, rows[LAYER_ROWS : 2 * LAYER_ROWS])
    send_a(3)
    send_a(4)
    send_strip(0, rows[0:LAYER_ROWS])
    send_strip(1, rows[LAYER_ROWS : 2 * LAYER_ROWS])

    sums = jnp.concatenate([arrived(1), arrived(2)], axis=0)
    high = sums.astype(BF16)
    low = (sums - high.astype(F32)).astype(BF16)
    grad_hidden = mid[...].astype(F32) + dot(spread[...], high) + dot(spread[...], low)
    gpre = (grad_hidden * deriv[...]).astype(BF16)
    put(5, rim_gradient(gpre, taps1, kt1, FIRST))
    send_a(5)
    kernel_gradient(0, x1f, gpre, FIRST)
    ar_core(0)

    center[...] = dot(shift2[...], hidden)
    lay(x2h, center[...])
    kernel_gradient(1, x2h, cot[...], SECOND)
    send_b(3)
    send_b(4)
    ar_scatter(0)
    slide_strips(0)
    slide_strips(1)
    sides = dot_first(slid[...], met_side[...])
    corners = dot_first(strip_in[:, 4].reshape(256, CH), met_corner[...])
    for j in range(4):
        pieces = [(CORNER_TAP[j], corners[:, j * CH : (j + 1) * CH])]
        for k, slide in enumerate(SLIDES):
            pieces.append((slide_tap(j, slide), sides[k * CH : (k + 1) * CH, j * CH : (j + 1) * CH]))
        for (a, b), piece in pieces:
            put_rows(1, (a * 3 + b) * CH, piece, add=True)
    ar_core(1)
    send_b(5)
    ar_scatter(1)
    lay(x1g, dot(shift1[...], gpre))
    mid[...] = conv(x1g, lambda a: kt1[a * 384 : (a + 1) * 384, :], FIRST).astype(BF16)
    send_line(3, 0)
    send_line(4, 3)
    ar_line(0)
    ar_line(1)
    send_line(5, 1)

    ar_gather(0)
    rims = jnp.concatenate([arrived(3), arrived(4)], axis=0).astype(BF16)
    lay(x2h, center[...] + dot(rim2[...], rims))
    out[...] = conv(x2h, lambda a: k2[a], SECOND).astype(BF16)
    stores = [
        pltpu.make_async_copy(out, out_hbm, store_sem.at[2]),
        pltpu.make_async_copy(fgrad, fgrad_hbm, store_sem.at[3]),
    ]
    stores[0].start()
    ar_gather(1)
    sums = arrived(5)
    high = sums.astype(BF16)
    low = (sums - high.astype(F32)).astype(BF16)
    fgrad[...] = (
        mid[...].astype(F32) + dot(spread[:, 0:LAYER_ROWS], high) + dot(spread[:, 0:LAYER_ROWS], low)
    ).astype(BF16)
    stores[1].start()
    ar_share(0)
    ar_share(1)
    for layer in range(LAYERS):
        finish_sends(layer)
    for depth in range(2):
        wait_bytes(strip_in.at[depth, :, pl.ds(0, 112), :], strip_sem.at[0, depth])
    for copy in stores:
        copy.wait()
    for which in range(2):
        ar_finish(which)
        ar_sent(which)


def store_kernel(out_in, fgrad_in, halves_in, out_to, fgrad_to, first_to, second_to, out, fgrad, halves, grads, sem):
    def load(i, src, dst):
        copy = pltpu.make_async_copy(src, dst, sem.at[0, i])
        copy.start()
        return copy

    def store(i, src, dst):
        copy = pltpu.make_async_copy(src, dst, sem.at[1, i])
        copy.start()
        return copy

    loads = [
        load(0, halves_in.at[1], halves.at[1]),
        load(1, halves_in.at[0], halves.at[0]),
        load(2, out_in, out),
        load(3, fgrad_in, fgrad),
    ]
    stores = []
    for k, which in enumerate((1, 0)):
        loads[k].wait()
        for i in range(16):
            at = i * CHUNK
            grads[which, at : at + HALF, :] = halves[which, 0, i].astype(F32)
            grads[which, at + HALF : at + CHUNK, :] = halves[which, 1, i].astype(F32)[2 * HALF - CHUNK : HALF]
        stores.append(store(k, grads.at[which], (first_to, second_to)[which]))
    loads[2].wait()
    stores.append(store(2, out, out_to))
    loads[3].wait()
    stores.append(store(3, fgrad, fgrad_to))
    for copy in stores:
        copy.wait()


def local(features, cotangent, kernel_first_layer, kernel_second_layer, neighbors, turns):
    operands = [
        features.reshape(PX, CH),
        cotangent.reshape(PX, CH),
        kernel_first_layer.reshape(3, 3 * CH, CH),
        kernel_second_layer.reshape(3, 3 * CH, CH),
        neighbors.T,
        turns.T,
    ] + constants()
    hbm = pl.BlockSpec(memory_space=pltpu.HBM)
    tile = jax.ShapeDtypeStruct((PX, CH), BF16)
    halves = jax.ShapeDtypeStruct((2, 2, 16, HALF, CH), BF16)
    grad = jax.ShapeDtypeStruct((9 * CH, CH), F32)
    results = pl.pallas_call(
        block_kernel,
        out_shape=(tile, tile, halves),
        in_specs=[hbm] * len(operands),
        out_specs=(hbm,) * 3,
        scratch_shapes=[pltpu.VMEM(x.shape, x.dtype) for x in operands]
        + [
            pltpu.VMEM((LAYERS, 5, 256, CH), BF16),
            pltpu.VMEM((6, 5, 128, CH), BF16),
            pltpu.VMEM((6, 5, 128, CH), BF16),
            pltpu.VMEM((4, 2, 128, PX), BF16),
            pltpu.VMEM((9 * CH, CH), BF16),
            pltpu.VMEM((9 * CH, CH), BF16),
            pltpu.VMEM((288, 3 * CH), BF16),
            pltpu.VMEM((288, 3 * CH), BF16),
            pltpu.VMEM((320, 3 * CH), BF16),
            pltpu.VMEM((320, 3 * CH), BF16),
            pltpu.VMEM((LAYER_ROWS, 9 * CH), BF16),
            pltpu.VMEM((3 * 320, CH), F32),
            pltpu.VMEM((PX, CH), BF16),
            pltpu.VMEM((PX, CH), F32),
            pltpu.VMEM((2, 5, 16, CH), BF16),
            pltpu.VMEM((2, 5, 128, CH), BF16),
            pltpu.VMEM((1024, 3 * CH), BF16),
            pltpu.VMEM((1024, 4 * CH), BF16),
            pltpu.VMEM((256, 4 * CH), BF16),
            pltpu.VMEM((4 * CH, 4 * CH), BF16),
            pltpu.VMEM((2, 16, CHUNK, CH), F32),
            pltpu.VMEM((2, 16, HALF, CH), F32),
            pltpu.VMEM((2, 16, HALF, CH), BF16),
            pltpu.VMEM((2, 16, HALF, CH), BF16),
            pltpu.VMEM((2, 4, HALF, CH), F32),
            pltpu.VMEM((2, 16, HALF, CH), BF16),
            pltpu.VMEM((PX, CH), BF16),
            pltpu.VMEM((PX, CH), BF16),
            pltpu.SemaphoreType.DMA((LAYERS, 3)),
            pltpu.SemaphoreType.DMA((LAYERS, 3)),
            pltpu.SemaphoreType.DMA((2, 5)),
            pltpu.SemaphoreType.DMA((2, 5)),
            pltpu.SemaphoreType.DMA((len(operands),)),
            pltpu.SemaphoreType.DMA((4,)),
            pltpu.SemaphoreType.DMA((2, 2)),
            pltpu.SemaphoreType.REGULAR,
        ],
        compiler_params=pltpu.CompilerParams(
            collective_id=0, has_side_effects=True, vmem_limit_bytes=60 * 2**20
        ),
    )(*operands)
    output, features_gradient, first, second = pl.pallas_call(
        store_kernel,
        out_shape=(tile, tile, grad, grad),
        in_specs=[hbm] * 3,
        out_specs=(hbm,) * 4,
        scratch_shapes=[
            pltpu.VMEM((PX, CH), BF16),
            pltpu.VMEM((PX, CH), BF16),
            pltpu.VMEM((2, 2, 16, HALF, CH), BF16),
            pltpu.VMEM((2, 9 * CH, CH), F32),
            pltpu.SemaphoreType.DMA((2, 4)),
        ],
        compiler_params=pltpu.CompilerParams(vmem_limit_bytes=60 * 2**20),
    )(*results)
    return (
        output.reshape(features.shape),
        features_gradient.reshape(features.shape),
        first.reshape(kernel_first_layer.shape),
        second.reshape(kernel_second_layer.shape),
    )


def solution(mesh):
    placed = (P("tile", None, None, None), P("tile", None, None, None), P(), P(), P(), P())
    return jax.shard_map(
        local,
        mesh=mesh,
        in_specs=placed,
        out_specs=(P("tile", None, None, None), P("tile", None, None, None), P(), P()),
        check_vma=False,
    )
```

```python
import functools
import math

import jax
import jax.numpy as jnp
import numpy as np
from jax import lax
from jax.experimental import pallas as pl
from jax.experimental.pallas import tpu as pltpu
from jax.sharding import PartitionSpec as P

SIDE = 16
PX = SIDE * SIDE
CH = 128
TILES = 128
FIRST, SECOND = 1, 2
SCALE = 1.0 / math.sqrt(TILES * PX)

gelu_scale = 0.7978845608028654
gelu_cubic = 0.044715

F32, BF16 = jnp.float32, jnp.bfloat16
MESH = pl.DeviceIdType.MESH

STRIDE = {"y": 32, "x": 8, "z": 2}
SHIFT = {"y": 5, "x": 3, "z": 1}
PLANS = (("x", "y", "z"), ("y", "z", "x"), ("z", "x", "y"))
LAYER_PLAN = (0, 1, 2, 0, 2, 1)
LAYERS = 6
SLICES = (4, 4, 4, 4, 4, 5)
CORNER_SLICE = (3, 0, 0, 3, 3, 4)

ROW_STEP = (-1, -1, 0, 1, 1, 1, 0, -1)
COL_STEP = (0, 1, 1, 1, 0, -1, -1, -1)

LAYER_ROWS = 80

FAR_FIRST = (2, 1, 3)

CHUNK, SENT = 72, 80
SUM_PLANS = (("z", "x", "y"), ("x", "y", "z"))


def side_pixel(j, depth, along):
    last = SIDE - 1
    return ((depth, along), (along, last - depth), (last - depth, last - along), (last - along, depth))[j]


def layer_rows(width):
    for q in range(5):
        for e in range(4):
            for j in range(4):
                row = q * 16 + e * 4 + j
                if q < 4:
                    yield row, 2 * j, 4 * q + e
                elif 2 - width <= e < 2:
                    yield row, 2 * j + 1, SIDE - 2 + e


def rim_place(d, depth, along, width):
    facing = (d + 4) % 8
    i, j = side_pixel(facing // 2, depth, along)
    return width + SIDE * ROW_STEP[d] + i, width + SIDE * COL_STEP[d] + j


def pick_matrix(depth):
    out = np.zeros((LAYER_ROWS, PX), np.float32)
    for row, compass, along in layer_rows(2):
        i, j = side_pixel(compass // 2, depth, along)
        out[row, i * SIDE + j] = 1
    return out


def shift_matrix(width):
    rows = SIDE + 2 * width
    out = np.zeros((3, rows, SIDE, PX), np.float32)
    for b in range(3):
        for i in range(SIDE):
            for j in range(SIDE):
                src = j + b * width - width
                if 0 <= src < SIDE:
                    out[b, i + width, j, i * SIDE + src] = 1
    return out.reshape(3 * rows * SIDE, PX)


def rim_matrix(width):
    rows = SIDE + 2 * width
    out = np.zeros((3, rows, SIDE, width * LAYER_ROWS), np.float32)
    for depth in range(width):
        for row, d, along in layer_rows(width):
            i, j = rim_place(d, depth, along, width)
            for b in range(3):
                col = j - b * width
                if 0 <= col < SIDE:
                    out[b, i, col, depth * LAYER_ROWS + row] = 1
    return out.reshape(3 * rows * SIDE, width * LAYER_ROWS)


def taps_matrix(width):
    out = np.zeros((3, 3, width * LAYER_ROWS, PX), np.float32)
    for depth in range(width):
        for row, d, along in layer_rows(width):
            i, j = rim_place(d, depth, along, width)
            for a in range(3):
                for b in range(3):
                    si, sj = i - width * (2 - a), j - width * (2 - b)
                    if 0 <= si < SIDE and 0 <= sj < SIDE:
                        out[a, b, depth * LAYER_ROWS + row, si * SIDE + sj] = 1
    return out.reshape(9 * width * LAYER_ROWS, PX)


SIDE_TAP = ((0, 1), (1, 2), (2, 1), (1, 0))
CORNER_TAP = ((0, 2), (2, 2), (2, 0), (0, 0))
SLIDES = (-2, 0, 2)


def met_pixel(d, depth, along, tap):
    i, j = rim_place(d, depth, along, 2)
    return i - 2 * tap[0], j - 2 * tap[1]


def met_matrix():
    out = np.zeros((2, LAYER_ROWS, PX), np.float32)
    for depth in range(2):
        for row, d, along in layer_rows(2):
            i, j = met_pixel(d, depth, along, CORNER_TAP[d // 2] if d % 2 else SIDE_TAP[d // 2])
            out[depth, row, i * SIDE + j] = 1
    return out.reshape(2 * LAYER_ROWS, PX)


def slide_tap(j, slide):
    target = met_pixel(2 * j, 0, 7 + slide, SIDE_TAP[j])
    return [(a, b) for a in range(3) for b in range(3) if met_pixel(2 * j, 0, 7, (a, b)) == target][0]


def constants():
    pick = np.concatenate([pick_matrix(0), pick_matrix(1)])
    arrays = (
        pick,
        np.ascontiguousarray(pick.T),
        shift_matrix(1),
        shift_matrix(2),
        rim_matrix(1),
        rim_matrix(2),
        taps_matrix(1),
        met_matrix(),
    )
    return [jnp.asarray(a, BF16) for a in arrays]


def dot(a, b):
    return jnp.dot(a, b, preferred_element_type=F32)


def dot_first(a, b):
    return lax.dot_general(a, b, (((0,), (0,)), ((), ())), preferred_element_type=F32)


def coordinate(index, axis):
    return (index >> SHIFT[axis]) & 3


def block_kernel(
    feat_in, cot_in, k1_in, k2_in, nb_in, turns_in,
    pick_in, spread_in, shift1_in, shift2_in, rim1_in, rim2_in, taps1_in, met_in,
    out_hbm, fgrad_hbm, sums_hbm,
    feat, cot, k1, k2, nb, turns, pick, spread, shift1, shift2, rim1, rim2, taps1, met,
    buf, msg, recv, choose, kt1, kt2, x1f, x1g, x2h, x2c, zcat, center, mid, deriv,
    strip, strip_in, slid, met_side, met_corner, tap_kernels,
    grads, core_in, part, rs_in, line_in, ag_in, out, fgrad,
    send_sem, recv_sem, ar_send, ar_recv, load_sem, store_sem, strip_sem, go_sem,
):
    me = lax.axis_index("tile")
    core = me & 1
    pos = {axis: coordinate(me, axis) for axis in "yxz"}

    def along(axis, i):
        return me + (((pos[axis] + i) & 3) - pos[axis]) * STRIDE[axis]

    def plane_peers(which):
        a, b, _ = SUM_PLANS[which]
        steps = [(da, db) for da in range(4) for db in range(4) if da or db]
        for da, db in sorted(steps, key=lambda step: -sum(min(d, 4 - d) for d in step)):
            at_a, at_b = (pos[a] + da) & 3, (pos[b] + db) & 3
            yield me + (at_a - pos[a]) * STRIDE[a] + (at_b - pos[b]) * STRIDE[b], at_b * 4 + at_a

    sibling = me + 1 - 2 * core

    peers = [sibling] + [along(axis, i) for axis in "xyz" for i in FAR_FIRST]
    barrier = pltpu.get_barrier_semaphore()
    for device in peers:
        pl.semaphore_signal(barrier, inc=1, device_id=(device,), device_id_type=MESH)

    loads = {}
    for i, (name, src, dst) in enumerate(
        (
            ("pick", pick_in, pick), ("feat", feat_in, feat), ("met", met_in, met), ("cot", cot_in, cot),
            ("k2", k2_in, k2), ("nb", nb_in, nb), ("turns", turns_in, turns),
            ("shift1", shift1_in, shift1), ("shift2", shift2_in, shift2), ("rim1", rim1_in, rim1),
            ("k1", k1_in, k1), ("spread", spread_in, spread), ("taps1", taps1_in, taps1), ("rim2", rim2_in, rim2),
        )
    ):
        loads[name] = pltpu.make_async_copy(src, dst, load_sem.at[i])
        loads[name].start()

    def loaded(*names):
        for name in names:
            loads[name].wait()

    def remote(src, dst, send, arrive, device):
        pltpu.make_async_remote_copy(
            src_ref=src, dst_ref=dst, send_sem=send, recv_sem=arrive, device_id=(device,), device_id_type=MESH
        ).start()

    def wait_bytes(ref, sem):
        pltpu.make_async_copy(ref, ref, sem).wait()

    def own_rows(layer):
        a, b, _ = PLANS[LAYER_PLAN[layer]]
        return pl.ds(pl.multiple_of((pos[b] * 4 + pos[a]) * 16, 16), 16)

    def put(layer, values):
        n = SLICES[layer]
        buf[layer, 0:n, own_rows(layer), :] = values[0 : n * 16].astype(BF16).reshape(n, 16, CH)

    def blocks(layer, count):
        return buf.at[layer, pl.ds(0, SLICES[layer]), pl.ds(0, count * 16), :]

    def send_a(layer):
        axis = PLANS[LAYER_PLAN[layer]][0]
        view = buf.at[layer, pl.ds(0, SLICES[layer]), own_rows(layer), :]
        for i in FAR_FIRST:
            remote(view, view, send_sem.at[layer, 0], recv_sem.at[layer, 0], along(axis, i))

    def gathered(layer):
        wait_bytes(blocks(layer, 12), recv_sem.at[layer, 1])

    def send_b(layer):
        axis = PLANS[LAYER_PLAN[layer]][1]
        wait_bytes(blocks(layer, 3), recv_sem.at[layer, 0])
        view = buf.at[layer, pl.ds(0, SLICES[layer]), pl.ds(pl.multiple_of(pos[axis] * 64, 64), 64), :]
        for i in FAR_FIRST:
            remote(view, view, send_sem.at[layer, 1], recv_sem.at[layer, 1], along(axis, i))

    def send_line(layer, chooser):
        gathered(layer)
        for q in range(5):
            source = buf[layer, q if q < 4 else CORNER_SLICE[layer]]
            msg[layer, q] = dot(choose[chooser, 0 if q < 4 else 1], source).astype(BF16)
        deliver(layer)

    def deliver(layer):
        axis = PLANS[LAYER_PLAN[layer]][2]
        mine = pl.ds(pl.multiple_of((pos[axis] * 2 + core) * 16, 16), 16)
        for i in FAR_FIRST + (0,):
            for flip in range(2):
                if i or flip:
                    other = core + flip - 2 * core * flip
                    device = along(axis, i) - core + other
                    theirs = pl.ds(pl.multiple_of((((pos[axis] + i) & 3) * 2 + other) * 16, 16), 16)
                    remote(
                        msg.at[layer, :, theirs, :], recv.at[layer, :, mine, :],
                        send_sem.at[layer, 2], recv_sem.at[layer, 2], device,
                    )
        recv[layer, :, mine, :] = msg[layer, :, mine, :]

    def send_strip(depth, values):
        axis = PLANS[LAYER_PLAN[1 + depth]][2]
        strip[depth] = values.astype(BF16).reshape(5, 16, CH)
        mine = pl.ds(pl.multiple_of((pos[axis] * 2 + core) * 16, 16), 16)
        for i in FAR_FIRST + (0,):
            for flip in range(2):
                if i or flip:
                    device = along(axis, i) + flip - 2 * core * flip
                    remote(
                        strip.at[depth], strip_in.at[depth, :, mine, :],
                        strip_sem.at[0, depth], strip_sem.at[1, depth], device,
                    )
        strip_in[depth, :, mine, :] = strip[depth]

    def meet(layer):
        gathered(layer)
        depth = layer - 1
        lane = lax.broadcasted_iota(jnp.int32, (128, PX), 1) & 3
        for corner in range(2):
            full = choose[layer, corner].astype(F32)
            split = jnp.concatenate([jnp.where(lane == j, full, 0.0).astype(BF16) for j in range(4)], axis=0)
            for q in (4,) if corner else range(4):
                found = dot(split, buf[layer, q if q < 4 else CORNER_SLICE[layer]]).astype(BF16)
                for j in range(4):
                    part_j = found[j * 128 : (j + 1) * 128]
                    if corner:
                        met_corner[depth * 128 : (depth + 1) * 128, j * CH : (j + 1) * CH] = part_j
                    else:
                        at = (depth * 4 + q) * 128
                        met_side[at : at + 128, j * CH : (j + 1) * CH] = part_j

    def slide(x, step):
        x = x.reshape(4, 8, 2, 8, CH)
        empty = jnp.zeros((1, 8, 1, 8, CH), F32)
        first, second = x[:, :, 0:1], x[:, :, 1:2]
        if step < 0:
            x = jnp.concatenate([jnp.concatenate([empty, second[0:3]], axis=0), first], axis=2)
        elif step > 0:
            x = jnp.concatenate([second, jnp.concatenate([first[1:4], empty], axis=0)], axis=2)
        return x.reshape(512, CH)

    def send_rim_gradient(layer):
        depth = layer - 1
        meet(layer)
        terms = dot(met_side[depth * 512 : (depth + 1) * 512, :], tap_kernels[:, 0 : 3 * CH])
        total = None
        for k, step in enumerate(SLIDES):
            term = slide(terms[:, k * CH : (k + 1) * CH], step)
            total = term if total is None else total + term
        msg[layer, 0:4] = total.astype(BF16).reshape(4, 128, CH)
        corner = dot(met_corner[depth * 128 : (depth + 1) * 128, :], tap_kernels[:, 3 * CH : 4 * CH])
        msg[layer, 4] = corner.astype(BF16)
        deliver(layer)

    def lay_taps():
        for j in range(4):
            taps = [slide_tap(j, step) for step in SLIDES] + [CORNER_TAP[j]]
            for k, (a, b) in enumerate(taps):
                at = ((2 - a) * 3 + 2 - b) * CH
                tap_kernels[j * CH : (j + 1) * CH, k * CH : (k + 1) * CH] = kt2[at : at + CH, :]

    def slide_strips(depth):
        wait_bytes(strip_in.at[depth, :, pl.ds(0, 112), :], strip_sem.at[1, depth])
        x = strip_in[depth, 0:4].astype(F32)
        for k, step in enumerate(SLIDES):
            slid[depth * 512 : (depth + 1) * 512, k * CH : (k + 1) * CH] = slide(x, -step).astype(BF16)

    def arrived(layer):
        wait_bytes(recv.at[layer, :, pl.ds(0, 112), :], recv_sem.at[layer, 2])
        total = recv[layer, :, 0:16, :].astype(F32)
        for g in range(1, 8):
            total += recv[layer, :, g * 16 : g * 16 + 16, :].astype(F32)
        return total.reshape(LAYER_ROWS, CH)

    def finish_sends(layer):
        wait_bytes(blocks(layer, 3), send_sem.at[layer, 0])
        wait_bytes(blocks(layer, 12), send_sem.at[layer, 1])
        wait_bytes(recv.at[layer, :, pl.ds(0, 112), :], send_sem.at[layer, 2])

    def table_rows(device_of_row, column_of_row):
        rows = device_of_row.shape[0]
        ids = lax.broadcasted_iota(jnp.int32, (rows, TILES), 1)
        hot = jnp.where(ids == device_of_row, 1.0, 0.0).astype(BF16)
        keep = lax.broadcasted_iota(jnp.int32, (rows, 8), 1) == column_of_row
        picked = []
        for table in (nb, turns):
            values = lax.dot_general(
                hot, table[...].astype(F32).astype(BF16), (((1,), (1,)), ((), ())), preferred_element_type=F32
            )
            values = jnp.sum(jnp.where(keep, values, 0.0), axis=1, keepdims=True)
            picked.append(values.astype(jnp.int32))
        return picked

    def build_forward(slot, plan):
        a, b, line = PLANS[plan]
        row = lax.broadcasted_iota(jnp.int32, (128, 1), 0)
        dest = me - core - pos[line] * STRIDE[line] + (row >> 5) * STRIDE[line] + ((row >> 4) & 1)
        e, j = (row >> 2) & 3, row & 3
        for corner in range(2):
            source, quarter = table_rows(dest, 2 * j + corner)
            here = (source >= 0) & (coordinate(source, line) == pos[line]) & ((source & 1) == core)
            place = (coordinate(source, b) * 4 + coordinate(source, a)) * 16 + e * 4 + ((j + 2 + quarter) & 3)
            if corner:
                here, place = here & (e < 2), place + 8
            place = jnp.where(here, place, -1)
            lanes = lax.broadcasted_iota(jnp.int32, (128, PX), 1)
            choose[slot, corner] = jnp.where(lanes == place, 1.0, 0.0).astype(BF16)

    def build_adjoint(slot, plan):
        a, b, line = PLANS[plan]
        row = lax.broadcasted_iota(jnp.int32, (PX, 1), 0)
        owner = (
            me - pos[a] * STRIDE[a] - pos[b] * STRIDE[b]
            + (row >> 6) * STRIDE[b] + ((row >> 4) & 3) * STRIDE[a]
        )
        e, j = (row >> 2) & 3, row & 3
        for corner in range(2):
            target, quarter = table_rows(owner, 2 * j + corner)
            here = (target >= 0) & (coordinate(target, a) == pos[a]) & (coordinate(target, b) == pos[b])
            place = (coordinate(target, line) * 2 + (target & 1)) * 16 + e * 4 + ((j + 2 + quarter) & 3)
            place = jnp.where(here, place, -1)
            lanes = lax.broadcasted_iota(jnp.int32, (PX, 128), 1)
            choose[slot, corner] = jnp.where(lanes == place, 1.0, 0.0).T.astype(BF16)

    def flip_kernel(kernel, dest):
        for a in range(3):
            for b in range(3):
                tap = kernel[2 - a, (2 - b) * CH : (3 - b) * CH, :]
                at = (a * 3 + b) * CH
                dest[at : at + CH, :] = tap.astype(F32).T.astype(BF16)

    def lay(dest, columns):
        rows = dest.shape[0]
        for b in range(3):
            dest[:, b * CH : (b + 1) * CH] = columns[b * rows : (b + 1) * rows].astype(BF16)

    def conv(x, kernel, dilation):
        total = None
        for a in range(3):
            window = x[a * dilation * SIDE : a * dilation * SIDE + PX, :]
            tap = dot(window, kernel(a))
            total = tap if total is None else total + tap
        return total

    def rim_gradient(values, taps, kernel_t, width):
        rows = width * LAYER_ROWS
        for tap in range(9):
            shifted = dot(taps[tap * rows : (tap + 1) * rows, :], values)
            zcat[0:rows, tap * CH : (tap + 1) * CH] = shifted.astype(BF16)
        return dot(zcat[0:rows, :], kernel_t[...])

    def put_rows(which, start, values, add=False):
        at = 0
        while at < values.shape[0]:
            i, row = divmod(start + at, CHUNK)
            size = min(CHUNK - row, values.shape[0] - at)
            piece = values[at : at + size]
            if add:
                piece = piece + grads[which, i, row : row + size, :]
            grads[which, i, row : row + size, :] = piece
            at += size

    def kernel_gradient(which, x, right, dilation):
        for a in range(3):
            window = x[a * dilation * SIDE : a * dilation * SIDE + PX, :]
            put_rows(which, a * 3 * CH, dot_first(window, right))

    owners = [pos[b] * 4 + pos[a] for a, b, _ in SUM_PLANS]

    def padded(chunk):
        return jnp.concatenate([chunk, jnp.zeros(chunk.shape[:-2] + (SENT - CHUNK, CH), F32)], axis=-2).astype(BF16)

    def ar_core(which):
        @pl.when(core != which)
        def _():
            remote(grads.at[which], core_in, ar_send.at[0], ar_recv.at[0], sibling)

    def ar_scatter(which):
        @pl.when(core == which)
        def _():
            wait_bytes(core_in, ar_recv.at[0])
            for i in range(16):
                part[i] = padded(grads[which, i] + core_in[i])
            for device, i in plane_peers(which):
                remote(part.at[i], rs_in.at[owners[which]], ar_send.at[1], ar_recv.at[1], device)
            rs_in[owners[which]] = part[owners[which]]

    def ar_line(which):
        axis = SUM_PLANS[which][2]

        @pl.when(core == which)
        def _():
            wait_bytes(rs_in.at[pl.ds(0, 15)], ar_recv.at[1])
            total = rs_in[0].astype(F32)
            for i in range(1, 16):
                total += rs_in[i].astype(F32)
            line_in[pos[axis]] = total[0:CHUNK]
            for i in FAR_FIRST:
                view = line_in.at[pos[axis]]
                remote(view, view, ar_send.at[2], ar_recv.at[2], along(axis, i))

    def ar_gather(which):
        @pl.when(core == which)
        def _():
            wait_bytes(line_in.at[pl.ds(0, 3)], ar_recv.at[2])
            total = ((line_in[0] + line_in[1]) + line_in[2]) + line_in[3]
            ag_in[owners[which]] = padded(total * SCALE)
            for device, _ in plane_peers(which):
                view = ag_in.at[owners[which]]
                remote(view, view, ar_send.at[3], ar_recv.at[3], device)

    def ar_share(which):
        @pl.when(core == which)
        def _():
            wait_bytes(ag_in.at[pl.ds(0, 15)], ar_recv.at[3])
            remote(ag_in, sums_hbm.at[which], ar_send.at[4], ar_recv.at[4], sibling)
            pltpu.make_async_copy(ag_in, sums_hbm.at[which], store_sem.at[0]).start()

    def ar_finish():
        wait_bytes(ag_in, ar_recv.at[4])
        wait_bytes(ag_in, store_sem.at[0])
        wait_bytes(core_in, ar_send.at[0])
        wait_bytes(rs_in.at[pl.ds(0, 15)], ar_send.at[1])
        wait_bytes(line_in.at[pl.ds(0, 3)], ar_send.at[2])
        wait_bytes(ag_in.at[pl.ds(0, 15)], ar_send.at[3])
        wait_bytes(ag_in, ar_send.at[4])

    loaded("pick", "feat")
    put(0, dot(pick[0:LAYER_ROWS, :], feat[...]))
    loaded("met", "cot")
    rows = dot(met[...], cot[...])
    put(1, rows[0:LAYER_ROWS])
    put(2, rows[LAYER_ROWS : 2 * LAYER_ROWS])
    pl.semaphore_wait(barrier, len(peers))
    pl.semaphore_signal(go_sem, inc=1, device_id=(sibling,), device_id_type=MESH)
    for layer in range(3):
        send_a(layer)
    loaded("nb", "turns", "shift1", "shift2")
    build_forward(0, 0)
    build_adjoint(1, 1)
    build_adjoint(2, 2)
    for layer in range(3):
        send_b(layer)
    loaded("k2")
    flip_kernel(k2, kt2)
    lay_taps()
    center[0 : 3 * 288, :] = dot(shift1[...], feat[...])
    lay(x2c, dot(shift2[...], cot[...]))
    mid[...] = conv(x2c, lambda a: kt2[a * 384 : (a + 1) * 384, :], SECOND).astype(BF16)
    loaded("k1", "rim1", "spread", "taps1", "rim2")
    flip_kernel(k1, kt1)
    build_forward(3, 2)
    pl.semaphore_wait(go_sem, 1)
    send_line(0, 0)
    send_rim_gradient(1)
    send_rim_gradient(2)

    lay(x1f, center[0 : 3 * 288, :] + dot(rim1[...], arrived(0).astype(BF16)))
    v = conv(x1f, lambda a: k1[a], FIRST)
    tangent = jnp.tanh(gelu_scale * (v + gelu_cubic * v * v * v))
    hidden = (0.5 * v * (1.0 + tangent)).astype(BF16)
    deriv[...] = 0.5 * (1.0 + tangent) + 0.5 * v * (1.0 - tangent * tangent) * gelu_scale * (
        1.0 + 3.0 * gelu_cubic * v * v
    )
    rows = dot(pick[...], hidden)
    put(3, rows[0:LAYER_ROWS])
    put(4, rows[LAYER_ROWS : 2 * LAYER_ROWS])
    send_a(3)
    send_a(4)
    send_strip(0, rows[0:LAYER_ROWS])
    send_strip(1, rows[LAYER_ROWS : 2 * LAYER_ROWS])

    sums = jnp.concatenate([arrived(1), arrived(2)], axis=0)
    high = sums.astype(BF16)
    low = (sums - high.astype(F32)).astype(BF16)
    grad_hidden = mid[...].astype(F32) + dot(spread[...], high) + dot(spread[...], low)
    gpre = (grad_hidden * deriv[...]).astype(BF16)
    put(5, rim_gradient(gpre, taps1, kt1, FIRST))
    send_a(5)
    kernel_gradient(0, x1f, gpre, FIRST)
    ar_core(0)

    center[...] = dot(shift2[...], hidden)
    lay(x2h, center[...])
    kernel_gradient(1, x2h, cot[...], SECOND)
    send_b(3)
    send_b(4)
    ar_scatter(0)
    slide_strips(0)
    slide_strips(1)
    sides = dot_first(slid[...], met_side[...])
    corners = dot_first(strip_in[:, 4].reshape(256, CH), met_corner[...])
    for j in range(4):
        pieces = [(CORNER_TAP[j], corners[:, j * CH : (j + 1) * CH])]
        for k, slide in enumerate(SLIDES):
            pieces.append((slide_tap(j, slide), sides[k * CH : (k + 1) * CH, j * CH : (j + 1) * CH]))
        for (a, b), piece in pieces:
            put_rows(1, (a * 3 + b) * CH, piece, add=True)
    ar_core(1)
    send_b(5)
    ar_scatter(1)
    lay(x1g, dot(shift1[...], gpre))
    mid[...] = conv(x1g, lambda a: kt1[a * 384 : (a + 1) * 384, :], FIRST).astype(BF16)
    send_line(3, 0)
    send_line(4, 3)
    ar_line(0)
    ar_line(1)
    send_line(5, 1)

    ar_gather(0)
    rims = jnp.concatenate([arrived(3), arrived(4)], axis=0).astype(BF16)
    lay(x2h, center[...] + dot(rim2[...], rims))
    out[...] = conv(x2h, lambda a: k2[a], SECOND).astype(BF16)
    stores = [
        pltpu.make_async_copy(out, out_hbm, store_sem.at[2]),
        pltpu.make_async_copy(fgrad, fgrad_hbm, store_sem.at[3]),
    ]
    stores[0].start()
    ar_gather(1)
    sums = arrived(5)
    high = sums.astype(BF16)
    low = (sums - high.astype(F32)).astype(BF16)
    fgrad[...] = (
        mid[...].astype(F32) + dot(spread[:, 0:LAYER_ROWS], high) + dot(spread[:, 0:LAYER_ROWS], low)
    ).astype(BF16)
    stores[1].start()
    ar_share(0)
    ar_share(1)
    for layer in range(LAYERS):
        finish_sends(layer)
    for depth in range(2):
        wait_bytes(strip_in.at[depth, :, pl.ds(0, 112), :], strip_sem.at[0, depth])
    for copy in stores:
        copy.wait()
    ar_finish()


def store_kernel(out_in, fgrad_in, sums_from, out_to, fgrad_to, first_to, second_to, out, fgrad, sums_in, grads, sem):
    def load(i, src, dst):
        copy = pltpu.make_async_copy(src, dst, sem.at[0, i])
        copy.start()
        return copy

    def store(i, src, dst):
        copy = pltpu.make_async_copy(src, dst, sem.at[1, i])
        copy.start()
        return copy

    loads = [
        load(0, sums_from.at[1], sums_in.at[1]),
        load(1, sums_from.at[0], sums_in.at[0]),
        load(2, out_in, out),
        load(3, fgrad_in, fgrad),
    ]
    stores = []
    for k, which in enumerate((1, 0)):
        loads[k].wait()
        for i in range(16):
            at = i * CHUNK
            grads[which, at : at + CHUNK, :] = sums_in[which, i].astype(F32)[0:CHUNK]
        stores.append(store(k, grads.at[which], (first_to, second_to)[which]))
    loads[2].wait()
    stores.append(store(2, out, out_to))
    loads[3].wait()
    stores.append(store(3, fgrad, fgrad_to))
    for copy in stores:
        copy.wait()


def local(features, cotangent, kernel_first_layer, kernel_second_layer, neighbors, turns):
    operands = [
        features.reshape(PX, CH),
        cotangent.reshape(PX, CH),
        kernel_first_layer.reshape(3, 3 * CH, CH),
        kernel_second_layer.reshape(3, 3 * CH, CH),
        neighbors.T,
        turns.T,
    ] + constants()
    hbm = pl.BlockSpec(memory_space=pltpu.HBM)
    tile = jax.ShapeDtypeStruct((PX, CH), BF16)
    sums_in = jax.ShapeDtypeStruct((2, 16, SENT, CH), BF16)
    grad = jax.ShapeDtypeStruct((9 * CH, CH), F32)
    results = pl.pallas_call(
        block_kernel,
        out_shape=(tile, tile, sums_in),
        in_specs=[hbm] * len(operands),
        out_specs=(hbm,) * 3,
        scratch_shapes=[pltpu.VMEM(x.shape, x.dtype) for x in operands]
        + [
            pltpu.VMEM((LAYERS, 5, 256, CH), BF16),
            pltpu.VMEM((6, 5, 128, CH), BF16),
            pltpu.VMEM((6, 5, 128, CH), BF16),
            pltpu.VMEM((4, 2, 128, PX), BF16),
            pltpu.VMEM((9 * CH, CH), BF16),
            pltpu.VMEM((9 * CH, CH), BF16),
            pltpu.VMEM((288, 3 * CH), BF16),
            pltpu.VMEM((288, 3 * CH), BF16),
            pltpu.VMEM((320, 3 * CH), BF16),
            pltpu.VMEM((320, 3 * CH), BF16),
            pltpu.VMEM((LAYER_ROWS, 9 * CH), BF16),
            pltpu.VMEM((3 * 320, CH), F32),
            pltpu.VMEM((PX, CH), BF16),
            pltpu.VMEM((PX, CH), F32),
            pltpu.VMEM((2, 5, 16, CH), BF16),
            pltpu.VMEM((2, 5, 128, CH), BF16),
            pltpu.VMEM((1024, 3 * CH), BF16),
            pltpu.VMEM((1024, 4 * CH), BF16),
            pltpu.VMEM((256, 4 * CH), BF16),
            pltpu.VMEM((4 * CH, 4 * CH), BF16),
            pltpu.VMEM((2, 16, CHUNK, CH), F32),
            pltpu.VMEM((16, CHUNK, CH), F32),
            pltpu.VMEM((16, SENT, CH), BF16),
            pltpu.VMEM((16, SENT, CH), BF16),
            pltpu.VMEM((4, CHUNK, CH), F32),
            pltpu.VMEM((16, SENT, CH), BF16),
            pltpu.VMEM((PX, CH), BF16),
            pltpu.VMEM((PX, CH), BF16),
            pltpu.SemaphoreType.DMA((LAYERS, 3)),
            pltpu.SemaphoreType.DMA((LAYERS, 3)),
            pltpu.SemaphoreType.DMA((5,)),
            pltpu.SemaphoreType.DMA((5,)),
            pltpu.SemaphoreType.DMA((len(operands),)),
            pltpu.SemaphoreType.DMA((4,)),
            pltpu.SemaphoreType.DMA((2, 2)),
            pltpu.SemaphoreType.REGULAR,
        ],
        compiler_params=pltpu.CompilerParams(
            collective_id=0, has_side_effects=True, vmem_limit_bytes=60 * 2**20
        ),
    )(*operands)
    output, features_gradient, first, second = pl.pallas_call(
        store_kernel,
        out_shape=(tile, tile, grad, grad),
        in_specs=[hbm] * 3,
        out_specs=(hbm,) * 4,
        scratch_shapes=[
            pltpu.VMEM((PX, CH), BF16),
            pltpu.VMEM((PX, CH), BF16),
            pltpu.VMEM((2, 16, SENT, CH), BF16),
            pltpu.VMEM((2, 9 * CH, CH), F32),
            pltpu.SemaphoreType.DMA((2, 4)),
        ],
        compiler_params=pltpu.CompilerParams(vmem_limit_bytes=60 * 2**20),
    )(*results)
    return (
        output.reshape(features.shape),
        features_gradient.reshape(features.shape),
        first.reshape(kernel_first_layer.shape),
        second.reshape(kernel_second_layer.shape),
    )


def solution(mesh):
    placed = (P("tile", None, None, None), P("tile", None, None, None), P(), P(), P(), P())
    return jax.shard_map(
        local,
        mesh=mesh,
        in_specs=placed,
        out_specs=(P("tile", None, None, None), P("tile", None, None, None), P(), P()),
        check_vma=False,
    )
```

```python
import functools
import math

import jax
import jax.numpy as jnp
import numpy as np
from jax import lax
from jax.experimental import pallas as pl
from jax.experimental.pallas import tpu as pltpu
from jax.sharding import PartitionSpec as P

SIDE = 16
PX = SIDE * SIDE
CH = 128
TILES = 128
FIRST, SECOND = 1, 2
SCALE = 1.0 / math.sqrt(TILES * PX)

gelu_scale = 0.7978845608028654
gelu_cubic = 0.044715

F32, BF16 = jnp.float32, jnp.bfloat16
MESH = pl.DeviceIdType.MESH

STRIDE = {"y": 32, "x": 8, "z": 2}
SHIFT = {"y": 5, "x": 3, "z": 1}
PLANS = (("x", "y", "z"), ("y", "z", "x"), ("z", "x", "y"))
LAYER_PLAN = (0, 1, 2, 0, 2, 1)
LAYERS = 6
SLICES = (4, 4, 4, 4, 4, 5)
CORNER_SLICE = (3, 0, 0, 3, 3, 4)

ROW_STEP = (-1, -1, 0, 1, 1, 1, 0, -1)
COL_STEP = (0, 1, 1, 1, 0, -1, -1, -1)

LAYER_ROWS = 80

FAR_FIRST = (2, 1, 3)

CHUNK, SENT = 72, 80
SUM_PLANS = (("z", "x", "y"), ("x", "y", "z"))


def side_pixel(j, depth, along):
    last = SIDE - 1
    return ((depth, along), (along, last - depth), (last - depth, last - along), (last - along, depth))[j]


def layer_rows(width):
    for q in range(5):
        for e in range(4):
            for j in range(4):
                row = q * 16 + e * 4 + j
                if q < 4:
                    yield row, 2 * j, 4 * q + e
                elif 2 - width <= e < 2:
                    yield row, 2 * j + 1, SIDE - 2 + e


def rim_place(d, depth, along, width):
    facing = (d + 4) % 8
    i, j = side_pixel(facing // 2, depth, along)
    return width + SIDE * ROW_STEP[d] + i, width + SIDE * COL_STEP[d] + j


def pick_matrix(depth):
    out = np.zeros((LAYER_ROWS, PX), np.float32)
    for row, compass, along in layer_rows(2):
        i, j = side_pixel(compass // 2, depth, along)
        out[row, i * SIDE + j] = 1
    return out


def shift_matrix(width):
    rows = SIDE + 2 * width
    out = np.zeros((3, rows, SIDE, PX), np.float32)
    for b in range(3):
        for i in range(SIDE):
            for j in range(SIDE):
                src = j + b * width - width
                if 0 <= src < SIDE:
                    out[b, i + width, j, i * SIDE + src] = 1
    return out.reshape(3 * rows * SIDE, PX)


def rim_matrix(width):
    rows = SIDE + 2 * width
    out = np.zeros((3, rows, SIDE, width * LAYER_ROWS), np.float32)
    for depth in range(width):
        for row, d, along in layer_rows(width):
            i, j = rim_place(d, depth, along, width)
            for b in range(3):
                col = j - b * width
                if 0 <= col < SIDE:
                    out[b, i, col, depth * LAYER_ROWS + row] = 1
    return out.reshape(3 * rows * SIDE, width * LAYER_ROWS)


def taps_matrix(width):
    out = np.zeros((3, 3, width * LAYER_ROWS, PX), np.float32)
    for depth in range(width):
        for row, d, along in layer_rows(width):
            i, j = rim_place(d, depth, along, width)
            for a in range(3):
                for b in range(3):
                    si, sj = i - width * (2 - a), j - width * (2 - b)
                    if 0 <= si < SIDE and 0 <= sj < SIDE:
                        out[a, b, depth * LAYER_ROWS + row, si * SIDE + sj] = 1
    return out.reshape(9 * width * LAYER_ROWS, PX)


SIDE_TAP = ((0, 1), (1, 2), (2, 1), (1, 0))
CORNER_TAP = ((0, 2), (2, 2), (2, 0), (0, 0))
SLIDES = (-2, 0, 2)


def met_pixel(d, depth, along, tap):
    i, j = rim_place(d, depth, along, 2)
    return i - 2 * tap[0], j - 2 * tap[1]


def met_matrix():
    out = np.zeros((2, LAYER_ROWS, PX), np.float32)
    for depth in range(2):
        for row, d, along in layer_rows(2):
            i, j = met_pixel(d, depth, along, CORNER_TAP[d // 2] if d % 2 else SIDE_TAP[d // 2])
            out[depth, row, i * SIDE + j] = 1
    return out.reshape(2 * LAYER_ROWS, PX)


def slide_tap(j, slide):
    target = met_pixel(2 * j, 0, 7 + slide, SIDE_TAP[j])
    return [(a, b) for a in range(3) for b in range(3) if met_pixel(2 * j, 0, 7, (a, b)) == target][0]


def constants():
    pick = np.concatenate([pick_matrix(0), pick_matrix(1)])
    arrays = (
        pick,
        np.ascontiguousarray(pick.T),
        shift_matrix(1),
        shift_matrix(2),
        rim_matrix(1),
        rim_matrix(2),
        taps_matrix(1),
        met_matrix(),
    )
    return [jnp.asarray(a, BF16) for a in arrays]


def dot(a, b):
    return jnp.dot(a, b, preferred_element_type=F32)


def dot_first(a, b):
    return lax.dot_general(a, b, (((0,), (0,)), ((), ())), preferred_element_type=F32)


def coordinate(index, axis):
    return (index >> SHIFT[axis]) & 3


def block_kernel(
    feat_in, cot_in, k1_in, k2_in, nb_in, turns_in,
    pick_in, spread_in, shift1_in, shift2_in, rim1_in, rim2_in, taps1_in, met_in,
    out_hbm, fgrad_hbm, sums_hbm,
    feat, cot, k1, k2, nb, turns, pick, spread, shift1, shift2, rim1, rim2, taps1, met,
    buf, msg, recv, choose, kt1, kt2, x1f, x1g, x2h, x2c, zcat, center, mid, deriv,
    strip, strip_in, slid, met_side, met_corner, tap_kernels,
    grads, core_in, part, rs_in, line_in, ag_in, out, fgrad,
    send_sem, recv_sem, ar_send, ar_recv, load_sem, store_sem, strip_sem, go_sem,
):
    me = lax.axis_index("tile")
    core = me & 1
    pos = {axis: coordinate(me, axis) for axis in "yxz"}

    def along(axis, i):
        return me + (((pos[axis] + i) & 3) - pos[axis]) * STRIDE[axis]

    def plane_peers(which):
        a, b, _ = SUM_PLANS[which]
        steps = [(da, db) for da in range(4) for db in range(4) if da or db]
        for da, db in sorted(steps, key=lambda step: -sum(min(d, 4 - d) for d in step)):
            at_a, at_b = (pos[a] + da) & 3, (pos[b] + db) & 3
            yield me + (at_a - pos[a]) * STRIDE[a] + (at_b - pos[b]) * STRIDE[b], at_b * 4 + at_a

    sibling = me + 1 - 2 * core

    peers = [sibling] + [along(axis, i) for axis in "xyz" for i in FAR_FIRST]
    barrier = pltpu.get_barrier_semaphore()
    for device in peers:
        pl.semaphore_signal(barrier, inc=1, device_id=(device,), device_id_type=MESH)

    loads = {}
    for i, (name, src, dst) in enumerate(
        (
            ("pick", pick_in, pick), ("feat", feat_in, feat), ("met", met_in, met), ("cot", cot_in, cot),
            ("k2", k2_in, k2), ("nb", nb_in, nb), ("turns", turns_in, turns),
            ("shift1", shift1_in, shift1), ("shift2", shift2_in, shift2), ("rim1", rim1_in, rim1),
            ("k1", k1_in, k1), ("spread", spread_in, spread), ("taps1", taps1_in, taps1), ("rim2", rim2_in, rim2),
        )
    ):
        loads[name] = pltpu.make_async_copy(src, dst, load_sem.at[i])
        loads[name].start()

    def loaded(*names):
        for name in names:
            loads[name].wait()

    def remote(src, dst, send, arrive, device):
        pltpu.make_async_remote_copy(
            src_ref=src, dst_ref=dst, send_sem=send, recv_sem=arrive, device_id=(device,), device_id_type=MESH
        ).start()

    def wait_bytes(ref, sem):
        pltpu.make_async_copy(ref, ref, sem).wait()

    def own_rows(layer):
        a, b, _ = PLANS[LAYER_PLAN[layer]]
        return pl.ds(pl.multiple_of((pos[b] * 4 + pos[a]) * 16, 16), 16)

    def put(layer, values):
        n = SLICES[layer]
        buf[layer, 0:n, own_rows(layer), :] = values[0 : n * 16].astype(BF16).reshape(n, 16, CH)

    def blocks(layer, count):
        return buf.at[layer, pl.ds(0, SLICES[layer]), pl.ds(0, count * 16), :]

    def send_a(layer):
        axis = PLANS[LAYER_PLAN[layer]][0]
        view = buf.at[layer, pl.ds(0, SLICES[layer]), own_rows(layer), :]
        for i in FAR_FIRST:
            remote(view, view, send_sem.at[layer, 0], recv_sem.at[layer, 0], along(axis, i))

    def gathered(layer):
        wait_bytes(blocks(layer, 12), recv_sem.at[layer, 1])

    def send_b(layer):
        axis = PLANS[LAYER_PLAN[layer]][1]
        wait_bytes(blocks(layer, 3), recv_sem.at[layer, 0])
        view = buf.at[layer, pl.ds(0, SLICES[layer]), pl.ds(pl.multiple_of(pos[axis] * 64, 64), 64), :]
        for i in FAR_FIRST:
            remote(view, view, send_sem.at[layer, 1], recv_sem.at[layer, 1], along(axis, i))

    def send_line(layer, chooser):
        gathered(layer)
        for q in range(5):
            source = buf[layer, q if q < 4 else CORNER_SLICE[layer]]
            msg[layer, q] = dot(choose[chooser, 0 if q < 4 else 1], source).astype(BF16)
        deliver(layer)

    def deliver(layer):
        axis = PLANS[LAYER_PLAN[layer]][2]
        mine = pl.ds(pl.multiple_of((pos[axis] * 2 + core) * 16, 16), 16)
        for i in FAR_FIRST + (0,):
            for flip in range(2):
                if i or flip:
                    other = core + flip - 2 * core * flip
                    device = along(axis, i) - core + other
                    theirs = pl.ds(pl.multiple_of((((pos[axis] + i) & 3) * 2 + other) * 16, 16), 16)
                    remote(
                        msg.at[layer, :, theirs, :], recv.at[layer, :, mine, :],
                        send_sem.at[layer, 2], recv_sem.at[layer, 2], device,
                    )
        recv[layer, :, mine, :] = msg[layer, :, mine, :]

    def send_strip(depth, values):
        axis = PLANS[LAYER_PLAN[1 + depth]][2]
        strip[depth] = values.astype(BF16).reshape(5, 16, CH)
        mine = pl.ds(pl.multiple_of((pos[axis] * 2 + core) * 16, 16), 16)
        for i in FAR_FIRST + (0,):
            for flip in range(2):
                if i or flip:
                    device = along(axis, i) + flip - 2 * core * flip
                    remote(
                        strip.at[depth], strip_in.at[depth, :, mine, :],
                        strip_sem.at[0, depth], strip_sem.at[1, depth], device,
                    )
        strip_in[depth, :, mine, :] = strip[depth]

    def meet(layer):
        gathered(layer)
        depth = layer - 1
        lane = lax.broadcasted_iota(jnp.int32, (128, PX), 1) & 3
        for corner in range(2):
            full = choose[layer, corner].astype(F32)
            split = jnp.concatenate([jnp.where(lane == j, full, 0.0).astype(BF16) for j in range(4)], axis=0)
            for q in (4,) if corner else range(4):
                found = dot(split, buf[layer, q if q < 4 else CORNER_SLICE[layer]]).astype(BF16)
                for j in range(4):
                    part_j = found[j * 128 : (j + 1) * 128]
                    if corner:
                        met_corner[depth * 128 : (depth + 1) * 128, j * CH : (j + 1) * CH] = part_j
                    else:
                        at = (depth * 4 + q) * 128
                        met_side[at : at + 128, j * CH : (j + 1) * CH] = part_j

    def slide(x, step):
        x = x.reshape(4, 8, 2, 8, CH)
        empty = jnp.zeros((1, 8, 1, 8, CH), F32)
        first, second = x[:, :, 0:1], x[:, :, 1:2]
        if step < 0:
            x = jnp.concatenate([jnp.concatenate([empty, second[0:3]], axis=0), first], axis=2)
        elif step > 0:
            x = jnp.concatenate([second, jnp.concatenate([first[1:4], empty], axis=0)], axis=2)
        return x.reshape(512, CH)

    def send_rim_gradient(layer):
        depth = layer - 1
        meet(layer)
        terms = dot(met_side[depth * 512 : (depth + 1) * 512, :], tap_kernels[:, 0 : 3 * CH])
        total = None
        for k, step in enumerate(SLIDES):
            term = slide(terms[:, k * CH : (k + 1) * CH], step)
            total = term if total is None else total + term
        msg[layer, 0:4] = total.astype(BF16).reshape(4, 128, CH)
        corner = dot(met_corner[depth * 128 : (depth + 1) * 128, :], tap_kernels[:, 3 * CH : 4 * CH])
        msg[layer, 4] = corner.astype(BF16)
        deliver(layer)

    def lay_taps():
        for j in range(4):
            taps = [slide_tap(j, step) for step in SLIDES] + [CORNER_TAP[j]]
            for k, (a, b) in enumerate(taps):
                at = ((2 - a) * 3 + 2 - b) * CH
                tap_kernels[j * CH : (j + 1) * CH, k * CH : (k + 1) * CH] = kt2[at : at + CH, :]

    def slide_strips(depth):
        wait_bytes(strip_in.at[depth, :, pl.ds(0, 112), :], strip_sem.at[1, depth])
        x = strip_in[depth, 0:4].astype(F32)
        for k, step in enumerate(SLIDES):
            slid[depth * 512 : (depth + 1) * 512, k * CH : (k + 1) * CH] = slide(x, -step).astype(BF16)

    def arrived(layer):
        wait_bytes(recv.at[layer, :, pl.ds(0, 112), :], recv_sem.at[layer, 2])
        total = recv[layer, :, 0:16, :].astype(F32)
        for g in range(1, 8):
            total += recv[layer, :, g * 16 : g * 16 + 16, :].astype(F32)
        return total.reshape(LAYER_ROWS, CH)

    def finish_sends(layer):
        wait_bytes(blocks(layer, 3), send_sem.at[layer, 0])
        wait_bytes(blocks(layer, 12), send_sem.at[layer, 1])
        wait_bytes(recv.at[layer, :, pl.ds(0, 112), :], send_sem.at[layer, 2])

    def table_rows(device_of_row, column_of_row):
        rows = device_of_row.shape[0]
        ids = lax.broadcasted_iota(jnp.int32, (rows, TILES), 1)
        hot = jnp.where(ids == device_of_row, 1.0, 0.0).astype(BF16)
        keep = lax.broadcasted_iota(jnp.int32, (rows, 8), 1) == column_of_row
        picked = []
        for table in (nb, turns):
            values = lax.dot_general(
                hot, table[...].astype(F32).astype(BF16), (((1,), (1,)), ((), ())), preferred_element_type=F32
            )
            values = jnp.sum(jnp.where(keep, values, 0.0), axis=1, keepdims=True)
            picked.append(values.astype(jnp.int32))
        return picked

    def build_forward(slot, plan):
        a, b, line = PLANS[plan]
        row = lax.broadcasted_iota(jnp.int32, (128, 1), 0)
        dest = me - core - pos[line] * STRIDE[line] + (row >> 5) * STRIDE[line] + ((row >> 4) & 1)
        e, j = (row >> 2) & 3, row & 3
        for corner in range(2):
            source, quarter = table_rows(dest, 2 * j + corner)
            here = (source >= 0) & (coordinate(source, line) == pos[line]) & ((source & 1) == core)
            place = (coordinate(source, b) * 4 + coordinate(source, a)) * 16 + e * 4 + ((j + 2 + quarter) & 3)
            if corner:
                here, place = here & (e < 2), place + 8
            place = jnp.where(here, place, -1)
            lanes = lax.broadcasted_iota(jnp.int32, (128, PX), 1)
            choose[slot, corner] = jnp.where(lanes == place, 1.0, 0.0).astype(BF16)

    def build_adjoint(slot, plan):
        a, b, line = PLANS[plan]
        row = lax.broadcasted_iota(jnp.int32, (PX, 1), 0)
        owner = (
            me - pos[a] * STRIDE[a] - pos[b] * STRIDE[b]
            + (row >> 6) * STRIDE[b] + ((row >> 4) & 3) * STRIDE[a]
        )
        e, j = (row >> 2) & 3, row & 3
        for corner in range(2):
            target, quarter = table_rows(owner, 2 * j + corner)
            here = (target >= 0) & (coordinate(target, a) == pos[a]) & (coordinate(target, b) == pos[b])
            place = (coordinate(target, line) * 2 + (target & 1)) * 16 + e * 4 + ((j + 2 + quarter) & 3)
            place = jnp.where(here, place, -1)
            lanes = lax.broadcasted_iota(jnp.int32, (PX, 128), 1)
            choose[slot, corner] = jnp.where(lanes == place, 1.0, 0.0).T.astype(BF16)

    def flip_kernel(kernel, dest):
        for a in range(3):
            for b in range(3):
                tap = kernel[2 - a, (2 - b) * CH : (3 - b) * CH, :]
                at = (a * 3 + b) * CH
                dest[at : at + CH, :] = tap.astype(F32).T.astype(BF16)

    def lay(dest, columns):
        rows = dest.shape[0]
        for b in range(3):
            dest[:, b * CH : (b + 1) * CH] = columns[b * rows : (b + 1) * rows].astype(BF16)

    def conv(x, kernel, dilation):
        total = None
        for a in range(3):
            window = x[a * dilation * SIDE : a * dilation * SIDE + PX, :]
            tap = dot(window, kernel(a))
            total = tap if total is None else total + tap
        return total

    def rim_gradient(values, taps, kernel_t, width):
        rows = width * LAYER_ROWS
        for tap in range(9):
            shifted = dot(taps[tap * rows : (tap + 1) * rows, :], values)
            zcat[0:rows, tap * CH : (tap + 1) * CH] = shifted.astype(BF16)
        return dot(zcat[0:rows, :], kernel_t[...])

    def put_rows(which, start, values, add=False):
        at = 0
        while at < values.shape[0]:
            i, row = divmod(start + at, CHUNK)
            size = min(CHUNK - row, values.shape[0] - at)
            piece = values[at : at + size]
            if add:
                piece = piece + grads[which, i, row : row + size, :]
            grads[which, i, row : row + size, :] = piece
            at += size

    def kernel_gradient(which, x, right, dilation):
        for a in range(3):
            window = x[a * dilation * SIDE : a * dilation * SIDE + PX, :]
            put_rows(which, a * 3 * CH, dot_first(window, right))

    owners = [pos[b] * 4 + pos[a] for a, b, _ in SUM_PLANS]

    def padded(chunk):
        return jnp.concatenate([chunk, jnp.zeros(chunk.shape[:-2] + (SENT - CHUNK, CH), F32)], axis=-2).astype(BF16)

    def ar_core(which):
        @pl.when(core != which)
        def _():
            remote(grads.at[which], core_in, ar_send.at[0], ar_recv.at[0], sibling)

    def ar_scatter(which):
        @pl.when(core == which)
        def _():
            wait_bytes(core_in, ar_recv.at[0])
            for i in range(16):
                part[i] = padded(grads[which, i] + core_in[i])
            for device, i in plane_peers(which):
                remote(part.at[i], rs_in.at[owners[which]], ar_send.at[1], ar_recv.at[1], device)
            rs_in[owners[which]] = part[owners[which]]

    def ar_line(which):
        axis = SUM_PLANS[which][2]

        @pl.when(core == which)
        def _():
            wait_bytes(rs_in.at[pl.ds(0, 15)], ar_recv.at[1])
            total = rs_in[0].astype(F32)
            for i in range(1, 16):
                total += rs_in[i].astype(F32)
            line_in[pos[axis]] = total[0:CHUNK]
            for i in FAR_FIRST:
                view = line_in.at[pos[axis]]
                remote(view, view, ar_send.at[2], ar_recv.at[2], along(axis, i))

    def ar_gather(which):
        @pl.when(core == which)
        def _():
            wait_bytes(line_in.at[pl.ds(0, 3)], ar_recv.at[2])
            total = ((line_in[0] + line_in[1]) + line_in[2]) + line_in[3]
            ag_in[owners[which]] = padded(total * SCALE)
            for device, _ in plane_peers(which):
                view = ag_in.at[owners[which]]
                remote(view, view, ar_send.at[3], ar_recv.at[3], device)

    def ar_share(which):
        @pl.when(core == which)
        def _():
            wait_bytes(ag_in.at[pl.ds(0, 15)], ar_recv.at[3])
            remote(ag_in, sums_hbm.at[which], ar_send.at[4], ar_recv.at[4], sibling)
            pltpu.make_async_copy(ag_in, sums_hbm.at[which], store_sem.at[0]).start()

    def ar_finish():
        wait_bytes(ag_in, ar_recv.at[4])
        wait_bytes(ag_in, store_sem.at[0])
        wait_bytes(core_in, ar_send.at[0])
        wait_bytes(rs_in.at[pl.ds(0, 15)], ar_send.at[1])
        wait_bytes(line_in.at[pl.ds(0, 3)], ar_send.at[2])
        wait_bytes(ag_in.at[pl.ds(0, 15)], ar_send.at[3])
        wait_bytes(ag_in, ar_send.at[4])

    loaded("pick", "feat")
    put(0, dot(pick[0:LAYER_ROWS, :], feat[...]))
    loaded("met", "cot")
    rows = dot(met[...], cot[...])
    put(1, rows[0:LAYER_ROWS])
    put(2, rows[LAYER_ROWS : 2 * LAYER_ROWS])
    pl.semaphore_wait(barrier, len(peers))
    pl.semaphore_signal(go_sem, inc=1, device_id=(sibling,), device_id_type=MESH)
    for layer in range(3):
        send_a(layer)
    loaded("nb", "turns", "shift1", "shift2")
    build_forward(0, 0)
    build_adjoint(1, 1)
    build_adjoint(2, 2)
    for layer in range(3):
        send_b(layer)
    loaded("k2")
    flip_kernel(k2, kt2)
    lay_taps()
    center[0 : 3 * 288, :] = dot(shift1[...], feat[...])
    lay(x2c, dot(shift2[...], cot[...]))
    mid[...] = conv(x2c, lambda a: kt2[a * 384 : (a + 1) * 384, :], SECOND).astype(BF16)
    loaded("k1", "rim1", "spread", "taps1", "rim2")
    flip_kernel(k1, kt1)
    build_forward(3, 2)
    pl.semaphore_wait(go_sem, 1)
    send_line(0, 0)
    send_rim_gradient(1)
    send_rim_gradient(2)

    lay(x1f, center[0 : 3 * 288, :] + dot(rim1[...], arrived(0).astype(BF16)))
    v = conv(x1f, lambda a: k1[a], FIRST)
    tangent = jnp.tanh(gelu_scale * (v + gelu_cubic * v * v * v))
    hidden = (0.5 * v * (1.0 + tangent)).astype(BF16)
    deriv[...] = 0.5 * (1.0 + tangent) + 0.5 * v * (1.0 - tangent * tangent) * gelu_scale * (
        1.0 + 3.0 * gelu_cubic * v * v
    )
    rows = dot(pick[...], hidden)
    put(3, rows[0:LAYER_ROWS])
    put(4, rows[LAYER_ROWS : 2 * LAYER_ROWS])
    send_a(3)
    send_a(4)
    send_strip(0, rows[0:LAYER_ROWS])
    send_strip(1, rows[LAYER_ROWS : 2 * LAYER_ROWS])

    center[...] = dot(shift2[...], hidden)
    lay(x2h, center[...])
    kernel_gradient(1, x2h, cot[...], SECOND)
    sums = jnp.concatenate([arrived(1), arrived(2)], axis=0)
    high = sums.astype(BF16)
    low = (sums - high.astype(F32)).astype(BF16)
    grad_hidden = mid[...].astype(F32) + dot(spread[...], high) + dot(spread[...], low)
    gpre = (grad_hidden * deriv[...]).astype(BF16)
    kernel_gradient(0, x1f, gpre, FIRST)
    ar_core(0)
    put(5, rim_gradient(gpre, taps1, kt1, FIRST))
    send_a(5)

    send_b(3)
    send_b(4)
    ar_scatter(0)
    slide_strips(0)
    slide_strips(1)
    sides = dot_first(slid[...], met_side[...])
    corners = dot_first(strip_in[:, 4].reshape(256, CH), met_corner[...])
    for j in range(4):
        pieces = [(CORNER_TAP[j], corners[:, j * CH : (j + 1) * CH])]
        for k, slide in enumerate(SLIDES):
            pieces.append((slide_tap(j, slide), sides[k * CH : (k + 1) * CH, j * CH : (j + 1) * CH]))
        for (a, b), piece in pieces:
            put_rows(1, (a * 3 + b) * CH, piece, add=True)
    ar_core(1)
    send_b(5)
    ar_scatter(1)
    lay(x1g, dot(shift1[...], gpre))
    mid[...] = conv(x1g, lambda a: kt1[a * 384 : (a + 1) * 384, :], FIRST).astype(BF16)
    send_line(3, 0)
    ar_line(0)
    send_line(4, 3)
    ar_line(1)
    send_line(5, 1)

    ar_gather(0)
    rims = jnp.concatenate([arrived(3), arrived(4)], axis=0).astype(BF16)
    lay(x2h, center[...] + dot(rim2[...], rims))
    out[...] = conv(x2h, lambda a: k2[a], SECOND).astype(BF16)
    stores = [
        pltpu.make_async_copy(out, out_hbm, store_sem.at[2]),
        pltpu.make_async_copy(fgrad, fgrad_hbm, store_sem.at[3]),
    ]
    stores[0].start()
    ar_gather(1)
    sums = arrived(5)
    high = sums.astype(BF16)
    low = (sums - high.astype(F32)).astype(BF16)
    fgrad[...] = (
        mid[...].astype(F32) + dot(spread[:, 0:LAYER_ROWS], high) + dot(spread[:, 0:LAYER_ROWS], low)
    ).astype(BF16)
    stores[1].start()
    ar_share(0)
    ar_share(1)
    for layer in range(LAYERS):
        finish_sends(layer)
    for depth in range(2):
        wait_bytes(strip_in.at[depth, :, pl.ds(0, 112), :], strip_sem.at[0, depth])
    for copy in stores:
        copy.wait()
    ar_finish()


def store_kernel(out_in, fgrad_in, sums_from, out_to, fgrad_to, first_to, second_to, out, fgrad, sums_in, grads, sem):
    def load(i, src, dst):
        copy = pltpu.make_async_copy(src, dst, sem.at[0, i])
        copy.start()
        return copy

    def store(i, src, dst):
        copy = pltpu.make_async_copy(src, dst, sem.at[1, i])
        copy.start()
        return copy

    loads = [
        load(0, sums_from.at[1], sums_in.at[1]),
        load(1, sums_from.at[0], sums_in.at[0]),
        load(2, out_in, out),
        load(3, fgrad_in, fgrad),
    ]
    stores = []
    for k, which in enumerate((1, 0)):
        loads[k].wait()
        for i in range(16):
            at = i * CHUNK
            grads[which, at : at + CHUNK, :] = sums_in[which, i].astype(F32)[0:CHUNK]
        stores.append(store(k, grads.at[which], (first_to, second_to)[which]))
    loads[2].wait()
    stores.append(store(2, out, out_to))
    loads[3].wait()
    stores.append(store(3, fgrad, fgrad_to))
    for copy in stores:
        copy.wait()


def local(features, cotangent, kernel_first_layer, kernel_second_layer, neighbors, turns):
    operands = [
        features.reshape(PX, CH),
        cotangent.reshape(PX, CH),
        kernel_first_layer.reshape(3, 3 * CH, CH),
        kernel_second_layer.reshape(3, 3 * CH, CH),
        neighbors.T,
        turns.T,
    ] + constants()
    hbm = pl.BlockSpec(memory_space=pltpu.HBM)
    tile = jax.ShapeDtypeStruct((PX, CH), BF16)
    sums_in = jax.ShapeDtypeStruct((2, 16, SENT, CH), BF16)
    grad = jax.ShapeDtypeStruct((9 * CH, CH), F32)
    results = pl.pallas_call(
        block_kernel,
        out_shape=(tile, tile, sums_in),
        in_specs=[hbm] * len(operands),
        out_specs=(hbm,) * 3,
        scratch_shapes=[pltpu.VMEM(x.shape, x.dtype) for x in operands]
        + [
            pltpu.VMEM((LAYERS, 5, 256, CH), BF16),
            pltpu.VMEM((6, 5, 128, CH), BF16),
            pltpu.VMEM((6, 5, 128, CH), BF16),
            pltpu.VMEM((4, 2, 128, PX), BF16),
            pltpu.VMEM((9 * CH, CH), BF16),
            pltpu.VMEM((9 * CH, CH), BF16),
            pltpu.VMEM((288, 3 * CH), BF16),
            pltpu.VMEM((288, 3 * CH), BF16),
            pltpu.VMEM((320, 3 * CH), BF16),
            pltpu.VMEM((320, 3 * CH), BF16),
            pltpu.VMEM((LAYER_ROWS, 9 * CH), BF16),
            pltpu.VMEM((3 * 320, CH), F32),
            pltpu.VMEM((PX, CH), BF16),
            pltpu.VMEM((PX, CH), F32),
            pltpu.VMEM((2, 5, 16, CH), BF16),
            pltpu.VMEM((2, 5, 128, CH), BF16),
            pltpu.VMEM((1024, 3 * CH), BF16),
            pltpu.VMEM((1024, 4 * CH), BF16),
            pltpu.VMEM((256, 4 * CH), BF16),
            pltpu.VMEM((4 * CH, 4 * CH), BF16),
            pltpu.VMEM((2, 16, CHUNK, CH), F32),
            pltpu.VMEM((16, CHUNK, CH), F32),
            pltpu.VMEM((16, SENT, CH), BF16),
            pltpu.VMEM((16, SENT, CH), BF16),
            pltpu.VMEM((4, CHUNK, CH), F32),
            pltpu.VMEM((16, SENT, CH), BF16),
            pltpu.VMEM((PX, CH), BF16),
            pltpu.VMEM((PX, CH), BF16),
            pltpu.SemaphoreType.DMA((LAYERS, 3)),
            pltpu.SemaphoreType.DMA((LAYERS, 3)),
            pltpu.SemaphoreType.DMA((5,)),
            pltpu.SemaphoreType.DMA((5,)),
            pltpu.SemaphoreType.DMA((len(operands),)),
            pltpu.SemaphoreType.DMA((4,)),
            pltpu.SemaphoreType.DMA((2, 2)),
            pltpu.SemaphoreType.REGULAR,
        ],
        compiler_params=pltpu.CompilerParams(
            collective_id=0, has_side_effects=True, vmem_limit_bytes=60 * 2**20
        ),
    )(*operands)
    output, features_gradient, first, second = pl.pallas_call(
        store_kernel,
        out_shape=(tile, tile, grad, grad),
        in_specs=[hbm] * 3,
        out_specs=(hbm,) * 4,
        scratch_shapes=[
            pltpu.VMEM((PX, CH), BF16),
            pltpu.VMEM((PX, CH), BF16),
            pltpu.VMEM((2, 16, SENT, CH), BF16),
            pltpu.VMEM((2, 9 * CH, CH), F32),
            pltpu.SemaphoreType.DMA((2, 4)),
        ],
        compiler_params=pltpu.CompilerParams(vmem_limit_bytes=60 * 2**20),
    )(*results)
    return (
        output.reshape(features.shape),
        features_gradient.reshape(features.shape),
        first.reshape(kernel_first_layer.shape),
        second.reshape(kernel_second_layer.shape),
    )


def solution(mesh):
    placed = (P("tile", None, None, None), P("tile", None, None, None), P(), P(), P(), P())
    return jax.shard_map(
        local,
        mesh=mesh,
        in_specs=placed,
        out_specs=(P("tile", None, None, None), P("tile", None, None, None), P(), P()),
        check_vma=False,
    )
```

```python
import functools
import math

import jax
import jax.numpy as jnp
import numpy as np
from jax import lax
from jax.experimental import pallas as pl
from jax.experimental.pallas import tpu as pltpu
from jax.sharding import PartitionSpec as P

SIDE = 16
PX = SIDE * SIDE
CH = 128
TILES = 128
FIRST, SECOND = 1, 2
SCALE = 1.0 / math.sqrt(TILES * PX)

gelu_scale = 0.7978845608028654
gelu_cubic = 0.044715

F32, BF16 = jnp.float32, jnp.bfloat16
MESH = pl.DeviceIdType.MESH

STRIDE = {"y": 32, "x": 8, "z": 2}
SHIFT = {"y": 5, "x": 3, "z": 1}
PLANS = (("x", "y", "z"), ("y", "z", "x"), ("z", "x", "y"))
LAYER_PLAN = (0, 1, 2, 0, 2, 1)
LAYERS = 6
SLICES = (4, 4, 4, 4, 4, 5)
CORNER_SLICE = (3, 0, 0, 3, 3, 4)

ROW_STEP = (-1, -1, 0, 1, 1, 1, 0, -1)
COL_STEP = (0, 1, 1, 1, 0, -1, -1, -1)

LAYER_ROWS = 80

FAR_FIRST = (2, 1, 3)

CHUNK, SENT = 72, 80
SUM_PLANS = (("z", "x", "y"), ("x", "y", "z"))


def side_pixel(j, depth, along):
    last = SIDE - 1
    return ((depth, along), (along, last - depth), (last - depth, last - along), (last - along, depth))[j]


def layer_rows(width):
    for q in range(5):
        for e in range(4):
            for j in range(4):
                row = q * 16 + e * 4 + j
                if q < 4:
                    yield row, 2 * j, 4 * q + e
                elif 2 - width <= e < 2:
                    yield row, 2 * j + 1, SIDE - 2 + e


def rim_place(d, depth, along, width):
    facing = (d + 4) % 8
    i, j = side_pixel(facing // 2, depth, along)
    return width + SIDE * ROW_STEP[d] + i, width + SIDE * COL_STEP[d] + j


def pick_matrix(depth):
    out = np.zeros((LAYER_ROWS, PX), np.float32)
    for row, compass, along in layer_rows(2):
        i, j = side_pixel(compass // 2, depth, along)
        out[row, i * SIDE + j] = 1
    return out


def shift_matrix(width):
    rows = SIDE + 2 * width
    out = np.zeros((3, rows, SIDE, PX), np.float32)
    for b in range(3):
        for i in range(SIDE):
            for j in range(SIDE):
                src = j + b * width - width
                if 0 <= src < SIDE:
                    out[b, i + width, j, i * SIDE + src] = 1
    return out.reshape(3 * rows * SIDE, PX)


def rim_matrix(width):
    rows = SIDE + 2 * width
    out = np.zeros((3, rows, SIDE, width * LAYER_ROWS), np.float32)
    for depth in range(width):
        for row, d, along in layer_rows(width):
            i, j = rim_place(d, depth, along, width)
            for b in range(3):
                col = j - b * width
                if 0 <= col < SIDE:
                    out[b, i, col, depth * LAYER_ROWS + row] = 1
    return out.reshape(3 * rows * SIDE, width * LAYER_ROWS)


def taps_matrix(width):
    out = np.zeros((3, 3, width * LAYER_ROWS, PX), np.float32)
    for depth in range(width):
        for row, d, along in layer_rows(width):
            i, j = rim_place(d, depth, along, width)
            for a in range(3):
                for b in range(3):
                    si, sj = i - width * (2 - a), j - width * (2 - b)
                    if 0 <= si < SIDE and 0 <= sj < SIDE:
                        out[a, b, depth * LAYER_ROWS + row, si * SIDE + sj] = 1
    return out.reshape(9 * width * LAYER_ROWS, PX)


SIDE_TAP = ((0, 1), (1, 2), (2, 1), (1, 0))
CORNER_TAP = ((0, 2), (2, 2), (2, 0), (0, 0))
SLIDES = (-2, 0, 2)


def met_pixel(d, depth, along, tap):
    i, j = rim_place(d, depth, along, 2)
    return i - 2 * tap[0], j - 2 * tap[1]


def met_matrix():
    out = np.zeros((2, LAYER_ROWS, PX), np.float32)
    for depth in range(2):
        for row, d, along in layer_rows(2):
            i, j = met_pixel(d, depth, along, CORNER_TAP[d // 2] if d % 2 else SIDE_TAP[d // 2])
            out[depth, row, i * SIDE + j] = 1
    return out.reshape(2 * LAYER_ROWS, PX)


def slide_tap(j, slide):
    target = met_pixel(2 * j, 0, 7 + slide, SIDE_TAP[j])
    return [(a, b) for a in range(3) for b in range(3) if met_pixel(2 * j, 0, 7, (a, b)) == target][0]


def constants():
    pick = np.concatenate([pick_matrix(0), pick_matrix(1)])
    arrays = (
        pick,
        np.ascontiguousarray(pick.T),
        shift_matrix(1),
        shift_matrix(2),
        rim_matrix(1),
        rim_matrix(2),
        taps_matrix(1),
        met_matrix(),
    )
    return [jnp.asarray(a, BF16) for a in arrays]


def dot(a, b):
    return jnp.dot(a, b, preferred_element_type=F32)


def dot_first(a, b):
    return lax.dot_general(a, b, (((0,), (0,)), ((), ())), preferred_element_type=F32)


def coordinate(index, axis):
    return (index >> SHIFT[axis]) & 3


def block_kernel(
    feat_in, cot_in, k1_in, k2_in, nb_in, turns_in,
    pick_in, spread_in, shift1_in, shift2_in, rim1_in, rim2_in, taps1_in, met_in,
    out_hbm, fgrad_hbm, sums_hbm,
    feat, cot, k1, k2, nb, turns, pick, spread, shift1, shift2, rim1, rim2, taps1, met,
    buf, msg, recv, choose, kt1, kt2, x1f, x1g, x2h, x2c, zcat, center, mid, deriv,
    strip, strip_in, slid, met_side, met_corner, tap_kernels,
    grads, core_in, part, rs_in, line_in, ag_in, out, fgrad,
    send_sem, recv_sem, ar_send, ar_recv, load_sem, store_sem, strip_sem, go_sem,
):
    me = lax.axis_index("tile")
    core = me & 1
    pos = {axis: coordinate(me, axis) for axis in "yxz"}

    def along(axis, i):
        return me + (((pos[axis] + i) & 3) - pos[axis]) * STRIDE[axis]

    def plane_peers(which):
        a, b, _ = SUM_PLANS[which]
        steps = [(da, db) for da in range(4) for db in range(4) if da or db]
        for da, db in sorted(steps, key=lambda step: -sum(min(d, 4 - d) for d in step)):
            at_a, at_b = (pos[a] + da) & 3, (pos[b] + db) & 3
            yield me + (at_a - pos[a]) * STRIDE[a] + (at_b - pos[b]) * STRIDE[b], at_b * 4 + at_a

    sibling = me + 1 - 2 * core

    peers = [sibling] + [along(axis, i) for axis in "xyz" for i in FAR_FIRST]
    barrier = pltpu.get_barrier_semaphore()
    for device in peers:
        pl.semaphore_signal(barrier, inc=1, device_id=(device,), device_id_type=MESH)

    loads = {}
    for i, (name, src, dst) in enumerate(
        (
            ("pick", pick_in, pick), ("feat", feat_in, feat), ("met", met_in, met), ("cot", cot_in, cot),
            ("k2", k2_in, k2), ("nb", nb_in, nb), ("turns", turns_in, turns),
            ("shift1", shift1_in, shift1), ("shift2", shift2_in, shift2), ("rim1", rim1_in, rim1),
            ("k1", k1_in, k1), ("spread", spread_in, spread), ("taps1", taps1_in, taps1), ("rim2", rim2_in, rim2),
        )
    ):
        loads[name] = pltpu.make_async_copy(src, dst, load_sem.at[i])
        loads[name].start()

    def loaded(*names):
        for name in names:
            loads[name].wait()

    def remote(src, dst, send, arrive, device):
        pltpu.make_async_remote_copy(
            src_ref=src, dst_ref=dst, send_sem=send, recv_sem=arrive, device_id=(device,), device_id_type=MESH
        ).start()

    def wait_bytes(ref, sem):
        pltpu.make_async_copy(ref, ref, sem).wait()

    def own_rows(layer):
        a, b, _ = PLANS[LAYER_PLAN[layer]]
        return pl.ds(pl.multiple_of((pos[b] * 4 + pos[a]) * 16, 16), 16)

    def put(layer, values):
        n = SLICES[layer]
        buf[layer, 0:n, own_rows(layer), :] = values[0 : n * 16].astype(BF16).reshape(n, 16, CH)

    def blocks(layer, count):
        return buf.at[layer, pl.ds(0, SLICES[layer]), pl.ds(0, count * 16), :]

    def send_a(layer):
        axis = PLANS[LAYER_PLAN[layer]][0]
        view = buf.at[layer, pl.ds(0, SLICES[layer]), own_rows(layer), :]
        for i in FAR_FIRST:
            remote(view, view, send_sem.at[layer, 0], recv_sem.at[layer, 0], along(axis, i))

    def gathered(layer):
        wait_bytes(blocks(layer, 12), recv_sem.at[layer, 1])

    def send_b(layer):
        axis = PLANS[LAYER_PLAN[layer]][1]
        wait_bytes(blocks(layer, 3), recv_sem.at[layer, 0])
        view = buf.at[layer, pl.ds(0, SLICES[layer]), pl.ds(pl.multiple_of(pos[axis] * 64, 64), 64), :]
        for i in FAR_FIRST:
            remote(view, view, send_sem.at[layer, 1], recv_sem.at[layer, 1], along(axis, i))

    def send_line(layer, chooser):
        gathered(layer)
        for q in range(5):
            source = buf[layer, q if q < 4 else CORNER_SLICE[layer]]
            msg[layer, q] = dot(choose[chooser, 0 if q < 4 else 1], source).astype(BF16)
        deliver(layer)

    def deliver(layer):
        axis = PLANS[LAYER_PLAN[layer]][2]
        mine = pl.ds(pl.multiple_of((pos[axis] * 2 + core) * 16, 16), 16)
        for i in FAR_FIRST + (0,):
            for flip in range(2):
                if i or flip:
                    other = core + flip - 2 * core * flip
                    device = along(axis, i) - core + other
                    theirs = pl.ds(pl.multiple_of((((pos[axis] + i) & 3) * 2 + other) * 16, 16), 16)
                    remote(
                        msg.at[layer, :, theirs, :], recv.at[layer, :, mine, :],
                        send_sem.at[layer, 2], recv_sem.at[layer, 2], device,
                    )
        recv[layer, :, mine, :] = msg[layer, :, mine, :]

    def send_strip(depth, values):
        axis = PLANS[LAYER_PLAN[1 + depth]][2]
        strip[depth] = values.astype(BF16).reshape(5, 16, CH)
        mine = pl.ds(pl.multiple_of((pos[axis] * 2 + core) * 16, 16), 16)
        for i in FAR_FIRST + (0,):
            for flip in range(2):
                if i or flip:
                    device = along(axis, i) + flip - 2 * core * flip
                    remote(
                        strip.at[depth], strip_in.at[depth, :, mine, :],
                        strip_sem.at[0, depth], strip_sem.at[1, depth], device,
                    )
        strip_in[depth, :, mine, :] = strip[depth]

    def meet(layer):
        gathered(layer)
        depth = layer - 1
        lane = lax.broadcasted_iota(jnp.int32, (128, PX), 1) & 3
        for corner in range(2):
            full = choose[layer, corner].astype(F32)
            split = jnp.concatenate([jnp.where(lane == j, full, 0.0).astype(BF16) for j in range(4)], axis=0)
            for q in (4,) if corner else range(4):
                found = dot(split, buf[layer, q if q < 4 else CORNER_SLICE[layer]]).astype(BF16)
                for j in range(4):
                    part_j = found[j * 128 : (j + 1) * 128]
                    if corner:
                        met_corner[depth * 128 : (depth + 1) * 128, j * CH : (j + 1) * CH] = part_j
                    else:
                        at = (depth * 4 + q) * 128
                        met_side[at : at + 128, j * CH : (j + 1) * CH] = part_j

    def slide(x, step):
        x = x.reshape(4, 8, 2, 8, CH)
        empty = jnp.zeros((1, 8, 1, 8, CH), F32)
        first, second = x[:, :, 0:1], x[:, :, 1:2]
        if step < 0:
            x = jnp.concatenate([jnp.concatenate([empty, second[0:3]], axis=0), first], axis=2)
        elif step > 0:
            x = jnp.concatenate([second, jnp.concatenate([first[1:4], empty], axis=0)], axis=2)
        return x.reshape(512, CH)

    def send_rim_gradient(layer):
        depth = layer - 1
        meet(layer)
        terms = dot(met_side[depth * 512 : (depth + 1) * 512, :], tap_kernels[:, 0 : 3 * CH])
        total = None
        for k, step in enumerate(SLIDES):
            term = slide(terms[:, k * CH : (k + 1) * CH], step)
            total = term if total is None else total + term
        msg[layer, 0:4] = total.astype(BF16).reshape(4, 128, CH)
        corner = dot(met_corner[depth * 128 : (depth + 1) * 128, :], tap_kernels[:, 3 * CH : 4 * CH])
        msg[layer, 4] = corner.astype(BF16)
        deliver(layer)

    def lay_taps():
        for j in range(4):
            taps = [slide_tap(j, step) for step in SLIDES] + [CORNER_TAP[j]]
            for k, (a, b) in enumerate(taps):
                at = ((2 - a) * 3 + 2 - b) * CH
                tap_kernels[j * CH : (j + 1) * CH, k * CH : (k + 1) * CH] = kt2[at : at + CH, :]

    def slide_strips(depth):
        wait_bytes(strip_in.at[depth, :, pl.ds(0, 112), :], strip_sem.at[1, depth])
        x = strip_in[depth, 0:4].astype(F32)
        for k, step in enumerate(SLIDES):
            slid[depth * 512 : (depth + 1) * 512, k * CH : (k + 1) * CH] = slide(x, -step).astype(BF16)

    def arrived(layer):
        wait_bytes(recv.at[layer, :, pl.ds(0, 112), :], recv_sem.at[layer, 2])
        total = recv[layer, :, 0:16, :].astype(F32)
        for g in range(1, 8):
            total += recv[layer, :, g * 16 : g * 16 + 16, :].astype(F32)
        return total.reshape(LAYER_ROWS, CH)

    def finish_sends(layer):
        wait_bytes(blocks(layer, 3), send_sem.at[layer, 0])
        wait_bytes(blocks(layer, 12), send_sem.at[layer, 1])
        wait_bytes(recv.at[layer, :, pl.ds(0, 112), :], send_sem.at[layer, 2])

    def table_rows(device_of_row, column_of_row):
        rows = device_of_row.shape[0]
        ids = lax.broadcasted_iota(jnp.int32, (rows, TILES), 1)
        hot = jnp.where(ids == device_of_row, 1.0, 0.0).astype(BF16)
        keep = lax.broadcasted_iota(jnp.int32, (rows, 8), 1) == column_of_row
        picked = []
        for table in (nb, turns):
            values = lax.dot_general(
                hot, table[...].astype(F32).astype(BF16), (((1,), (1,)), ((), ())), preferred_element_type=F32
            )
            values = jnp.sum(jnp.where(keep, values, 0.0), axis=1, keepdims=True)
            picked.append(values.astype(jnp.int32))
        return picked

    def build_forward(slot, plan):
        a, b, line = PLANS[plan]
        row = lax.broadcasted_iota(jnp.int32, (128, 1), 0)
        dest = me - core - pos[line] * STRIDE[line] + (row >> 5) * STRIDE[line] + ((row >> 4) & 1)
        e, j = (row >> 2) & 3, row & 3
        for corner in range(2):
            source, quarter = table_rows(dest, 2 * j + corner)
            here = (source >= 0) & (coordinate(source, line) == pos[line]) & ((source & 1) == core)
            place = (coordinate(source, b) * 4 + coordinate(source, a)) * 16 + e * 4 + ((j + 2 + quarter) & 3)
            if corner:
                here, place = here & (e < 2), place + 8
            place = jnp.where(here, place, -1)
            lanes = lax.broadcasted_iota(jnp.int32, (128, PX), 1)
            choose[slot, corner] = jnp.where(lanes == place, 1.0, 0.0).astype(BF16)

    def build_adjoint(slot, plan):
        a, b, line = PLANS[plan]
        row = lax.broadcasted_iota(jnp.int32, (PX, 1), 0)
        owner = (
            me - pos[a] * STRIDE[a] - pos[b] * STRIDE[b]
            + (row >> 6) * STRIDE[b] + ((row >> 4) & 3) * STRIDE[a]
        )
        e, j = (row >> 2) & 3, row & 3
        for corner in range(2):
            target, quarter = table_rows(owner, 2 * j + corner)
            here = (target >= 0) & (coordinate(target, a) == pos[a]) & (coordinate(target, b) == pos[b])
            place = (coordinate(target, line) * 2 + (target & 1)) * 16 + e * 4 + ((j + 2 + quarter) & 3)
            place = jnp.where(here, place, -1)
            lanes = lax.broadcasted_iota(jnp.int32, (PX, 128), 1)
            choose[slot, corner] = jnp.where(lanes == place, 1.0, 0.0).T.astype(BF16)

    def flip_kernel(kernel, dest):
        for a in range(3):
            for b in range(3):
                tap = kernel[2 - a, (2 - b) * CH : (3 - b) * CH, :]
                at = (a * 3 + b) * CH
                dest[at : at + CH, :] = tap.astype(F32).T.astype(BF16)

    def lay(dest, columns):
        rows = dest.shape[0]
        for b in range(3):
            dest[:, b * CH : (b + 1) * CH] = columns[b * rows : (b + 1) * rows].astype(BF16)

    def conv(x, kernel, dilation):
        total = None
        for a in range(3):
            window = x[a * dilation * SIDE : a * dilation * SIDE + PX, :]
            tap = dot(window, kernel(a))
            total = tap if total is None else total + tap
        return total

    def rim_gradient(values, taps, kernel_t, width):
        rows = width * LAYER_ROWS
        for tap in range(9):
            shifted = dot(taps[tap * rows : (tap + 1) * rows, :], values)
            zcat[0:rows, tap * CH : (tap + 1) * CH] = shifted.astype(BF16)
        return dot(zcat[0:rows, :], kernel_t[...])

    def put_rows(which, start, values, add=False):
        at = 0
        while at < values.shape[0]:
            i, row = divmod(start + at, CHUNK)
            size = min(CHUNK - row, values.shape[0] - at)
            piece = values[at : at + size]
            if add:
                piece = piece + grads[which, i, row : row + size, :]
            grads[which, i, row : row + size, :] = piece
            at += size

    def kernel_gradient(which, x, right, dilation):
        for a in range(3):
            window = x[a * dilation * SIDE : a * dilation * SIDE + PX, :]
            put_rows(which, a * 3 * CH, dot_first(window, right))

    owners = [pos[b] * 4 + pos[a] for a, b, _ in SUM_PLANS]

    def padded(chunk):
        return jnp.concatenate([chunk, jnp.zeros(chunk.shape[:-2] + (SENT - CHUNK, CH), F32)], axis=-2).astype(BF16)

    def ar_core(which):
        @pl.when(core != which)
        def _():
            remote(grads.at[which], core_in, ar_send.at[0], ar_recv.at[0], sibling)

    def ar_scatter(which):
        @pl.when(core == which)
        def _():
            wait_bytes(core_in, ar_recv.at[0])
            for i in range(16):
                part[i] = padded(grads[which, i] + core_in[i])
            for device, i in plane_peers(which):
                remote(part.at[i], rs_in.at[owners[which]], ar_send.at[1], ar_recv.at[1], device)
            rs_in[owners[which]] = part[owners[which]]

    def ar_line(which):
        axis = SUM_PLANS[which][2]

        @pl.when(core == which)
        def _():
            wait_bytes(rs_in.at[pl.ds(0, 15)], ar_recv.at[1])
            total = rs_in[0].astype(F32)
            for i in range(1, 16):
                total += rs_in[i].astype(F32)
            line_in[pos[axis]] = total[0:CHUNK]
            for i in FAR_FIRST:
                view = line_in.at[pos[axis]]
                remote(view, view, ar_send.at[2], ar_recv.at[2], along(axis, i))

    def ar_gather(which):
        @pl.when(core == which)
        def _():
            wait_bytes(line_in.at[pl.ds(0, 3)], ar_recv.at[2])
            total = ((line_in[0] + line_in[1]) + line_in[2]) + line_in[3]
            ag_in[owners[which]] = padded(total * SCALE)
            for device, _ in plane_peers(which):
                view = ag_in.at[owners[which]]
                remote(view, view, ar_send.at[3], ar_recv.at[3], device)

    def ar_share(which):
        @pl.when(core == which)
        def _():
            wait_bytes(ag_in.at[pl.ds(0, 15)], ar_recv.at[3])
            remote(ag_in, sums_hbm.at[which], ar_send.at[4], ar_recv.at[4], sibling)
            pltpu.make_async_copy(ag_in, sums_hbm.at[which], store_sem.at[0]).start()

    def ar_finish():
        wait_bytes(ag_in, ar_recv.at[4])
        wait_bytes(ag_in, store_sem.at[0])
        wait_bytes(core_in, ar_send.at[0])
        wait_bytes(rs_in.at[pl.ds(0, 15)], ar_send.at[1])
        wait_bytes(line_in.at[pl.ds(0, 3)], ar_send.at[2])
        wait_bytes(ag_in.at[pl.ds(0, 15)], ar_send.at[3])
        wait_bytes(ag_in, ar_send.at[4])

    loaded("pick", "feat")
    put(0, dot(pick[0:LAYER_ROWS, :], feat[...]))
    loaded("met", "cot")
    rows = dot(met[...], cot[...])
    put(1, rows[0:LAYER_ROWS])
    put(2, rows[LAYER_ROWS : 2 * LAYER_ROWS])
    pl.semaphore_wait(barrier, len(peers))
    pl.semaphore_signal(go_sem, inc=1, device_id=(sibling,), device_id_type=MESH)
    for layer in range(3):
        send_a(layer)
    loaded("nb", "turns", "shift1", "shift2")
    build_forward(0, 0)
    build_adjoint(1, 1)
    build_adjoint(2, 2)
    for layer in range(3):
        send_b(layer)
    loaded("k2")
    flip_kernel(k2, kt2)
    lay_taps()
    center[0 : 3 * 288, :] = dot(shift1[...], feat[...])
    lay(x2c, dot(shift2[...], cot[...]))
    mid[...] = conv(x2c, lambda a: kt2[a * 384 : (a + 1) * 384, :], SECOND).astype(BF16)
    loaded("k1", "rim1", "spread", "taps1", "rim2")
    flip_kernel(k1, kt1)
    build_forward(3, 2)
    pl.semaphore_wait(go_sem, 1)
    send_line(0, 0)
    send_rim_gradient(1)
    send_rim_gradient(2)

    lay(x1f, center[0 : 3 * 288, :] + dot(rim1[...], arrived(0).astype(BF16)))
    v = conv(x1f, lambda a: k1[a], FIRST)
    tangent = jnp.tanh(gelu_scale * (v + gelu_cubic * v * v * v))
    hidden = (0.5 * v * (1.0 + tangent)).astype(BF16)
    deriv[...] = 0.5 * (1.0 + tangent) + 0.5 * v * (1.0 - tangent * tangent) * gelu_scale * (
        1.0 + 3.0 * gelu_cubic * v * v
    )
    rows = dot(pick[...], hidden)
    put(3, rows[0:LAYER_ROWS])
    put(4, rows[LAYER_ROWS : 2 * LAYER_ROWS])
    send_a(3)
    send_a(4)
    send_strip(0, rows[0:LAYER_ROWS])
    send_strip(1, rows[LAYER_ROWS : 2 * LAYER_ROWS])

    center[...] = dot(shift2[...], hidden)
    lay(x2h, center[...])
    kernel_gradient(1, x2h, cot[...], SECOND)
    sums = jnp.concatenate([arrived(1), arrived(2)], axis=0)
    high = sums.astype(BF16)
    low = (sums - high.astype(F32)).astype(BF16)
    grad_hidden = mid[...].astype(F32) + dot(spread[...], high) + dot(spread[...], low)
    gpre = (grad_hidden * deriv[...]).astype(BF16)
    kernel_gradient(0, x1f, gpre, FIRST)
    ar_core(0)
    put(5, rim_gradient(gpre, taps1, kt1, FIRST))
    send_a(5)

    send_b(3)
    send_b(4)
    ar_scatter(0)
    slide_strips(0)
    slide_strips(1)
    sides = dot_first(slid[...], met_side[...])
    corners = dot_first(strip_in[:, 4].reshape(256, CH), met_corner[...])
    for j in range(4):
        pieces = [(CORNER_TAP[j], corners[:, j * CH : (j + 1) * CH])]
        for k, slide in enumerate(SLIDES):
            pieces.append((slide_tap(j, slide), sides[k * CH : (k + 1) * CH, j * CH : (j + 1) * CH]))
        for (a, b), piece in pieces:
            put_rows(1, (a * 3 + b) * CH, piece, add=True)
    ar_core(1)
    send_b(5)
    ar_scatter(1)
    lay(x1g, dot(shift1[...], gpre))
    mid[...] = conv(x1g, lambda a: kt1[a * 384 : (a + 1) * 384, :], FIRST).astype(BF16)
    send_line(3, 0)
    ar_line(0)
    send_line(4, 3)
    ar_line(1)
    send_line(5, 1)

    ar_gather(0)
    ar_gather(1)
    rims = jnp.concatenate([arrived(3), arrived(4)], axis=0).astype(BF16)
    lay(x2h, center[...] + dot(rim2[...], rims))
    out[...] = conv(x2h, lambda a: k2[a], SECOND).astype(BF16)
    stores = [
        pltpu.make_async_copy(out, out_hbm, store_sem.at[2]),
        pltpu.make_async_copy(fgrad, fgrad_hbm, store_sem.at[3]),
    ]
    stores[0].start()
    sums = arrived(5)
    high = sums.astype(BF16)
    low = (sums - high.astype(F32)).astype(BF16)
    fgrad[...] = (
        mid[...].astype(F32) + dot(spread[:, 0:LAYER_ROWS], high) + dot(spread[:, 0:LAYER_ROWS], low)
    ).astype(BF16)
    stores[1].start()
    ar_share(0)
    ar_share(1)
    for layer in range(LAYERS):
        finish_sends(layer)
    for depth in range(2):
        wait_bytes(strip_in.at[depth, :, pl.ds(0, 112), :], strip_sem.at[0, depth])
    for copy in stores:
        copy.wait()
    ar_finish()


def store_kernel(out_in, fgrad_in, sums_from, out_to, fgrad_to, first_to, second_to, out, fgrad, sums_in, grads, sem):
    def load(i, src, dst):
        copy = pltpu.make_async_copy(src, dst, sem.at[0, i])
        copy.start()
        return copy

    def store(i, src, dst):
        copy = pltpu.make_async_copy(src, dst, sem.at[1, i])
        copy.start()
        return copy

    loads = [
        load(0, sums_from.at[1], sums_in.at[1]),
        load(1, sums_from.at[0], sums_in.at[0]),
        load(2, out_in, out),
        load(3, fgrad_in, fgrad),
    ]
    stores = []
    for k, which in enumerate((1, 0)):
        loads[k].wait()
        for i in range(16):
            at = i * CHUNK
            grads[which, at : at + CHUNK, :] = sums_in[which, i].astype(F32)[0:CHUNK]
        stores.append(store(k, grads.at[which], (first_to, second_to)[which]))
    loads[2].wait()
    stores.append(store(2, out, out_to))
    loads[3].wait()
    stores.append(store(3, fgrad, fgrad_to))
    for copy in stores:
        copy.wait()


def local(features, cotangent, kernel_first_layer, kernel_second_layer, neighbors, turns):
    operands = [
        features.reshape(PX, CH),
        cotangent.reshape(PX, CH),
        kernel_first_layer.reshape(3, 3 * CH, CH),
        kernel_second_layer.reshape(3, 3 * CH, CH),
        neighbors.T,
        turns.T,
    ] + constants()
    hbm = pl.BlockSpec(memory_space=pltpu.HBM)
    tile = jax.ShapeDtypeStruct((PX, CH), BF16)
    sums_in = jax.ShapeDtypeStruct((2, 16, SENT, CH), BF16)
    grad = jax.ShapeDtypeStruct((9 * CH, CH), F32)
    results = pl.pallas_call(
        block_kernel,
        out_shape=(tile, tile, sums_in),
        in_specs=[hbm] * len(operands),
        out_specs=(hbm,) * 3,
        scratch_shapes=[pltpu.VMEM(x.shape, x.dtype) for x in operands]
        + [
            pltpu.VMEM((LAYERS, 5, 256, CH), BF16),
            pltpu.VMEM((6, 5, 128, CH), BF16),
            pltpu.VMEM((6, 5, 128, CH), BF16),
            pltpu.VMEM((4, 2, 128, PX), BF16),
            pltpu.VMEM((9 * CH, CH), BF16),
            pltpu.VMEM((9 * CH, CH), BF16),
            pltpu.VMEM((288, 3 * CH), BF16),
            pltpu.VMEM((288, 3 * CH), BF16),
            pltpu.VMEM((320, 3 * CH), BF16),
            pltpu.VMEM((320, 3 * CH), BF16),
            pltpu.VMEM((LAYER_ROWS, 9 * CH), BF16),
            pltpu.VMEM((3 * 320, CH), F32),
            pltpu.VMEM((PX, CH), BF16),
            pltpu.VMEM((PX, CH), F32),
            pltpu.VMEM((2, 5, 16, CH), BF16),
            pltpu.VMEM((2, 5, 128, CH), BF16),
            pltpu.VMEM((1024, 3 * CH), BF16),
            pltpu.VMEM((1024, 4 * CH), BF16),
            pltpu.VMEM((256, 4 * CH), BF16),
            pltpu.VMEM((4 * CH, 4 * CH), BF16),
            pltpu.VMEM((2, 16, CHUNK, CH), F32),
            pltpu.VMEM((16, CHUNK, CH), F32),
            pltpu.VMEM((16, SENT, CH), BF16),
            pltpu.VMEM((16, SENT, CH), BF16),
            pltpu.VMEM((4, CHUNK, CH), F32),
            pltpu.VMEM((16, SENT, CH), BF16),
            pltpu.VMEM((PX, CH), BF16),
            pltpu.VMEM((PX, CH), BF16),
            pltpu.SemaphoreType.DMA((LAYERS, 3)),
            pltpu.SemaphoreType.DMA((LAYERS, 3)),
            pltpu.SemaphoreType.DMA((5,)),
            pltpu.SemaphoreType.DMA((5,)),
            pltpu.SemaphoreType.DMA((len(operands),)),
            pltpu.SemaphoreType.DMA((4,)),
            pltpu.SemaphoreType.DMA((2, 2)),
            pltpu.SemaphoreType.REGULAR,
        ],
        compiler_params=pltpu.CompilerParams(
            collective_id=0, has_side_effects=True, vmem_limit_bytes=60 * 2**20
        ),
    )(*operands)
    output, features_gradient, first, second = pl.pallas_call(
        store_kernel,
        out_shape=(tile, tile, grad, grad),
        in_specs=[hbm] * 3,
        out_specs=(hbm,) * 4,
        scratch_shapes=[
            pltpu.VMEM((PX, CH), BF16),
            pltpu.VMEM((PX, CH), BF16),
            pltpu.VMEM((2, 16, SENT, CH), BF16),
            pltpu.VMEM((2, 9 * CH, CH), F32),
            pltpu.SemaphoreType.DMA((2, 4)),
        ],
        compiler_params=pltpu.CompilerParams(vmem_limit_bytes=60 * 2**20),
    )(*results)
    return (
        output.reshape(features.shape),
        features_gradient.reshape(features.shape),
        first.reshape(kernel_first_layer.shape),
        second.reshape(kernel_second_layer.shape),
    )


def solution(mesh):
    placed = (P("tile", None, None, None), P("tile", None, None, None), P(), P(), P(), P())
    return jax.shard_map(
        local,
        mesh=mesh,
        in_specs=placed,
        out_specs=(P("tile", None, None, None), P("tile", None, None, None), P(), P()),
        check_vma=False,
    )
```
